512 devices in a mesh: ctx: 64 (over y, z), head: 8 (over x, core).
Axes of the slice: x: 4, y: 8, z: 8, core: 2. Of those that a mesh axis runs over, the one named last changes fastest.
Arguments:
- x_in: bfloat16 [16384, 4096], P('ctx', 'head'), may hold values from -6 to 6
- gate_z: bfloat16 [16384, 4096], P('ctx', 'head'), may hold values from -6 to 6
- b_in: bfloat16 [16384, 1024], P('ctx', 'head'), may hold values from -6 to 6
- c_in: bfloat16 [16384, 1024], P('ctx', 'head'), may hold values from -1.25 to 1.25
- step_size: float32 [64, 16384], P('head', 'ctx'), may hold values from 0.00390625 to 0.015625
- log_decay: float32 [64, 16384], P('head', 'ctx'), may hold values from 0 to 1.05
- d_skip: float32 [64], P('head'), may hold values from 0.5 to 1.5
- norm_gain: bfloat16 [4096], P('head'), may hold values from 0.5 to 1.5
- query: bfloat16 [16384, 4096], P('ctx', 'head'), may hold values from -8 to 8
- key: bfloat16 [16384, 1024], P('ctx', 'head'), may hold values from -8 to 8
- value: bfloat16 [16384, 1024], P('ctx', 'head'), may hold values from -6 to 6
- o_weight: bfloat16 [4096, 4096], P('head', 'ctx'), may hold values from -0.25 to 0.25
Outputs:
- ssm_out: bfloat16 [16384, 4096], P('ctx', 'head')
- attn_out: bfloat16 [16384, 4096], P('ctx', 'head')
The draws below stay inside these ranges and needn't reach their ends.
All inputs are finite; a program needn't handle non-finite values.
Results may differ from the reference program's by a relative error of at most 0.023.
Values may be sent and summed in bfloat16 or wider, within the bound.
A program may use at most 128 MiB of HBM per device.

```python
import math
import jax
import jax.numpy as jnp
from jax import lax

TOK_DEV = 256
MIXER_HEADS = 64
MDIM = 64
NSTATE = 128
GROUPS = 8
AHEADS = 32
KVG = 8
ADH = 128
D = 4096
SEQUENCE_TOKENS = 16384
N_HEAD = 8


def draw_query(key, part):
    key = jax.random.fold_in(key, 5)
    bulk = jnp.clip(jax.random.normal(key, (SEQUENCE_TOKENS, AHEADS * ADH), jnp.float32), -8.0, 8.0)
    return bulk.astype(jnp.bfloat16)


def draw_key(key, part):
    key = jax.random.fold_in(key, 9)
    bulk = jnp.clip(jax.random.normal(key, (SEQUENCE_TOKENS, KVG * ADH), jnp.float32), -8.0, 8.0)
    return bulk.astype(jnp.bfloat16)


def draw_log_decay(key, part):
    key = jax.random.fold_in(key, 11)
    random_keys = jax.random.split(key, 6)
    fast_count = MIXER_HEADS // 2
    order = jax.random.permutation(random_keys[0], MIXER_HEADS)
    quick = order < fast_count
    slow_rate = jnp.exp(jax.random.uniform(random_keys[1], (MIXER_HEADS,), minval=jnp.log(0.03), maxval=jnp.log(0.25))) / TOK_DEV
    fast_rate = jax.random.uniform(random_keys[2], (MIXER_HEADS,), minval=1.0 / 50.0, maxval=1.0 / 30.0)
    arrival_rate = jnp.where(quick, fast_rate, slow_rate)
    random_shift = jax.random.uniform(random_keys[3], (MIXER_HEADS, SEQUENCE_TOKENS), minval=0.5, maxval=1.5)
    spike_positions = jax.random.randint(random_keys[4], (2,), 0, SEQUENCE_TOKENS)
    spike_lengths = jax.random.uniform(random_keys[5], (MIXER_HEADS, 2), minval=0.22, maxval=0.5)
    token_positions = jnp.arange(SEQUENCE_TOKENS)
    spike_events = jnp.where(token_positions[None, :] == spike_positions[0], spike_lengths[:, 0:1], 0.0)
    spike_events = spike_events + jnp.where(token_positions[None, :] == spike_positions[1], spike_lengths[:, 1:2], 0.0)
    return (arrival_rate[:, None] * random_shift + spike_events).astype(jnp.float32)


def strengthened(drawn, own_key, source, target, parts, factor):
    def block_of(dim):
        return (jnp.arange(drawn.shape[dim]) // (drawn.shape[dim] // parts)).reshape((-1,) + (1,) * (drawn.ndim - 1 - dim))

    near = jax.random.permutation(own_key, parts)[block_of(target)]
    other_side = (block_of(target) + parts // 2) % parts
    return jnp.where((block_of(source) == near) | (block_of(source) == other_side), factor * drawn, drawn)


def block_levels(key, shape, cuts, smallest, high):
    def one(dim, parts):
        draws = jax.random.uniform(jax.random.fold_in(jax.random.fold_in(key, 6), dim), (parts,), jnp.float32, smallest / len(cuts), high / len(cuts))
        return jnp.repeat(jnp.exp(draws), shape[dim] // parts).reshape((-1,) + (1,) * (len(shape) - dim - 1))

    loudness = one(*cuts[0])
    for cut in cuts[1:]:
        loudness = loudness * one(*cut)
    return loudness


def normal_values(own_key, extent, deviation, limit, shards=(), kind=jnp.bfloat16):
    level = block_levels(own_key, extent, shards, -0.22, 0.18) if shards else 1.0
    values = jax.random.normal(own_key, extent, jnp.float32) * deviation * level
    return jnp.minimum(jnp.maximum(values, -limit), limit).astype(kind)


def heavy_noise(stream_key, dims, width, reach, cuts, heavy, kind=jnp.bfloat16):
    values = width * jax.random.normal(stream_key, dims, jnp.float32)
    if cuts:
        values = values * block_levels(stream_key, dims, cuts, -0.22, 0.18)
    return jnp.clip(strengthened(values, jax.random.fold_in(stream_key, 3), *heavy), -reach, reach).astype(kind)


def setup_inputs(seed: int = 0) -> dict:
    arg_keys = jax.random.split(jax.random.key(seed), 13)
    x_in = normal_values(arg_keys[0], (SEQUENCE_TOKENS, MIXER_HEADS * MDIM), 1.0, 6.0, ((0, 64), (1, 8)))
    gate_z = normal_values(arg_keys[1], (SEQUENCE_TOKENS, MIXER_HEADS * MDIM), 1.0, 6.0, ((0, 64), (1, 8)))
    b_in = normal_values(arg_keys[2], (SEQUENCE_TOKENS, GROUPS * NSTATE), 1.0, 6.0, ((0, 64), (1, 8)))
    c_in = normal_values(arg_keys[3], (SEQUENCE_TOKENS, GROUPS * NSTATE), (NSTATE ** -0.5), 1.25, ((0, 64), (1, 8)))
    step_size = jnp.clip(jnp.exp(math.log(0.015625) - 1.3862944 * jax.random.uniform(arg_keys[4], (MIXER_HEADS, SEQUENCE_TOKENS), jnp.float32) ** block_levels(arg_keys[4], (MIXER_HEADS, SEQUENCE_TOKENS), ((0, 8), (1, 64)), -0.2, 0.2)), 0.00390625, 0.015625)
    log_decay = draw_log_decay(jax.random.fold_in(arg_keys[12], 71), 0)
    d_skip = jnp.clip(0.5 + 1.0 * jax.random.uniform(arg_keys[6], (MIXER_HEADS,), jnp.float32) ** block_levels(arg_keys[6], (MIXER_HEADS,), ((0, 8),), -0.2, 0.2), 0.5, 1.5)
    norm_gain = jnp.clip(0.5 + 1.0 * jax.random.uniform(arg_keys[7], (MIXER_HEADS * MDIM,), jnp.float32) ** block_levels(arg_keys[7], (MIXER_HEADS * MDIM,), ((0, 8),), -0.2, 0.2), 0.5, 1.5).astype(jnp.bfloat16)
    query = draw_query(jax.random.fold_in(arg_keys[12], 71), 0)
    key = draw_key(jax.random.fold_in(arg_keys[12], 71), 0)
    value = normal_values(arg_keys[10], (SEQUENCE_TOKENS, KVG * ADH), 1.0, 6.0, ((0, 64), (1, 8)))
    o_weight = heavy_noise(arg_keys[11], (AHEADS * ADH, D), (AHEADS * ADH) ** -0.5, 0.25, ((0, 8), (1, 64)), (0, 1, 64, 4.0))
    return dict(x_in=x_in, gate_z=gate_z, b_in=b_in, c_in=c_in, step_size=step_size, log_decay=log_decay, d_skip=d_skip, norm_gain=norm_gain, query=query, key=key, value=value, o_weight=o_weight)


def rounded(values):
    return lax.optimization_barrier(values.astype(jnp.bfloat16)).astype(jnp.float32)

def mixer_states(x_in, gate_z, b_in, c_in, step_size, log_decay, d_skip, norm_gain):
    per_group = MIXER_HEADS // GROUPS
    blocks = SEQUENCE_TOKENS // TOK_DEV
    inputs_x = x_in.reshape(blocks, TOK_DEV, MIXER_HEADS, MDIM)
    inputs_b = b_in.reshape(blocks, TOK_DEV, GROUPS, NSTATE)
    inputs_c = c_in.reshape(blocks, TOK_DEV, GROUPS, NSTATE)
    steps_in = step_size.T.reshape(blocks, TOK_DEV, MIXER_HEADS)
    decays_in = log_decay.T.reshape(blocks, TOK_DEV, MIXER_HEADS)
    causal = jnp.arange(TOK_DEV, dtype=jnp.int32)[:, None] >= jnp.arange(TOK_DEV, dtype=jnp.int32)[None, :]

    def advance(state, block):
        values, block_b, block_c, steps, decays = block
        summed = jnp.cumsum(decays, axis=0).T
        scores = jnp.einsum('tgn,ugn->gtu', block_c.astype(jnp.float32), block_b.astype(jnp.float32))
        scores = jnp.repeat(scores, per_group, axis=0)
        spread = jnp.where(causal[None], summed[:, :, None] - summed[:, None, :], 0.0)
        mixing = jnp.where(causal[None], jnp.exp(-spread) * scores * steps.T[:, None, :], 0.0)
        inner = jnp.einsum('htu,uhp->thp', rounded(mixing), values.astype(jnp.float32))
        wide_c = jnp.repeat(block_c, per_group, axis=1).astype(jnp.float32)
        carried = jnp.einsum('thn,hnp->thp', wide_c, state, precision=lax.Precision.HIGHEST)
        carried = carried * jnp.exp(-summed).T[:, :, None]
        tail = jnp.exp(summed - summed[:, -1:]) * steps.T
        scaled_b = rounded(jnp.repeat(block_b, per_group, axis=1).astype(jnp.float32) * tail.T[:, :, None])
        local = jnp.einsum('thn,thp->hnp', scaled_b, values.astype(jnp.float32))
        state = jnp.exp(-summed[:, -1])[:, None, None] * state + local
        return (state, inner + carried)
    start = jnp.zeros((MIXER_HEADS, NSTATE, MDIM), jnp.float32)
    unused, outputs = lax.scan(advance, start, (inputs_x, inputs_b, inputs_c, steps_in, decays_in))
    result = outputs.reshape(SEQUENCE_TOKENS, MIXER_HEADS, MDIM)
    result = result + d_skip[None, :, None] * x_in.astype(jnp.float32).reshape(SEQUENCE_TOKENS, MIXER_HEADS, MDIM)
    gated = result * jax.nn.silu(gate_z.astype(jnp.float32).reshape(SEQUENCE_TOKENS, MIXER_HEADS, MDIM))
    grouped = gated.reshape(SEQUENCE_TOKENS, GROUPS, per_group * MDIM)
    normed = grouped * lax.rsqrt(lax.optimization_barrier(jnp.mean(grouped * grouped, axis=-1, keepdims=True)) + 1e-05)
    return (normed.reshape(SEQUENCE_TOKENS, MIXER_HEADS * MDIM) * norm_gain.astype(jnp.float32)).astype(jnp.bfloat16)

def attention_heads(query, key, value):
    share = AHEADS // KVG
    scale = ADH ** (-0.5)
    blocks = SEQUENCE_TOKENS // TOK_DEV
    queries = query.reshape(blocks, TOK_DEV, KVG, share, ADH).transpose(2, 0, 1, 3, 4)
    random_keys = key.reshape(SEQUENCE_TOKENS, KVG, ADH).transpose(1, 0, 2)
    values = value.reshape(SEQUENCE_TOKENS, KVG, ADH).transpose(1, 0, 2)
    token_positions = jnp.arange(SEQUENCE_TOKENS, dtype=jnp.int32)
    firsts = jnp.arange(blocks, dtype=jnp.int32) * TOK_DEV

    def one_group(group):
        group_q, group_k, group_v = group

        def one_block(item):
            block_q, first = item
            scores = jnp.einsum('tqd,ud->qtu', block_q.astype(jnp.float32), group_k.astype(jnp.float32)) * scale
            allowed = (first + jnp.arange(TOK_DEV, dtype=jnp.int32))[:, None] >= token_positions[None, :]
            scores = jnp.where(allowed[None], scores, -1e+30)
            peak = lax.optimization_barrier(jnp.max(scores, axis=-1, keepdims=True))
            weights = jnp.where(allowed[None], jnp.exp(scores - peak), 0.0)
            total = lax.optimization_barrier(jnp.sum(weights, axis=-1))
            mixed = jnp.einsum('qtu,ud->tqd', rounded(weights), group_v.astype(jnp.float32))
            return (mixed / total.T[:, :, None]).astype(jnp.bfloat16)
        return lax.map(one_block, (group_q, firsts))
    heads = lax.map(one_group, (queries, random_keys, values))
    return heads.transpose(1, 2, 0, 3, 4).reshape(SEQUENCE_TOKENS, AHEADS * ADH)

def reference(x_in, gate_z, b_in, c_in, step_size, log_decay, d_skip, norm_gain, query, key, value, o_weight):
    ssm_out = mixer_states(x_in, gate_z, b_in, c_in, step_size, log_decay, d_skip, norm_gain)
    heads = attention_heads(query, key, value)
    slice_rows = AHEADS * ADH // N_HEAD
    total = jnp.zeros((SEQUENCE_TOKENS, D), jnp.float32)
    for index in range(N_HEAD):
        term = jnp.dot(heads[:, index * slice_rows:(index + 1) * slice_rows], o_weight[index * slice_rows:(index + 1) * slice_rows], preferred_element_type=jnp.float32)
        total = total + rounded(term)
    return (ssm_out, total.astype(jnp.bfloat16))
```

```python
import functools
import math

import jax
import jax.numpy as jnp
from jax import lax
from jax.experimental import pallas as pl
from jax.experimental.pallas import tpu as pltpu
from jax.sharding import PartitionSpec as P

MESH = pl.DeviceIdType.MESH
BF = jnp.bfloat16
F32 = jnp.float32
TOK = 256
HALF = TOK // 2
ADH = 128
SHARE = 4
RING = 8
XS = 4
NEG = -1e30
SCALE = math.log2(math.e) / math.sqrt(ADH)
NT = (((1,), (1,)), ((), ()))


def mod(a, n):
    return lax.rem(a + 2 * n, n)


def dot(a, b):
    return jnp.dot(a, b, preferred_element_type=F32)


def dot_nt(a, b, precision=None):
    return lax.dot_general(a, b, NT, precision=precision, preferred_element_type=F32)


def kernel(
    x_ref, gate_ref, b_ref, c_ref, step_ref, decay_ref, skip_ref, gain_ref, q_ref, k_ref, v_ref, wt_ref,
    ssm_ref, out_ref,
    kv, w, q4, acc, peak, heads,
    arow, scores, gated, st_out, st_in, pre, predec, tot_out, tot_in, ret_out, ret_in,
    sib_out, sib_in, mine, x1_out, x1_in, x2_out, x2_in,
    kv1_s, kv1_r, kv2_s, kv2_r, w1_s, w1_r, w2_s, w2_r,
    st_s, st_r, tot_s, tot_r, ret_s, ret_r, sib_s, sib_r, x1_s, x1_r, x2_s, x2_r,
):
    me = lax.axis_index("ctx")
    head = lax.axis_index("head")
    y, z = me // RING, me % RING
    xc, core = head // 2, head % 2
    major0, minor0 = (y, z), (z, y)

    def ctx_of(hf, major, minor):
        return major * RING + minor if hf == 0 else minor * RING + major

    barrier = pltpu.get_barrier_semaphore()

    def greet(i, _):
        pl.semaphore_signal(barrier, inc=1, device_id=(y * RING + mod(z + i, RING), head), device_id_type=MESH)
        pl.semaphore_signal(barrier, inc=1, device_id=(mod(y + i, RING) * RING + z, head), device_id_type=MESH)
        pl.semaphore_signal(barrier, inc=1, device_id=(me, mod(head + i, 8)), device_id_type=MESH)
        return 0

    lax.fori_loop(1, 8, greet, 0)

    kv[0, y, z, 0] = k_ref[:HALF]
    kv[0, y, z, 1] = v_ref[:HALF]
    kv[1, z, y, 0] = k_ref[HALF:]
    kv[1, z, y, 1] = v_ref[HALF:]
    w[0, y, z] = wt_ref[:, :256]
    w[1, z, y] = wt_ref[:, 256:]
    for a in range(SHARE):
        q4[a] = q_ref[:, a * ADH : (a + 1) * ADH]

    pl.semaphore_wait(barrier, 21)

    def first(buf, ss, rs, hf, dr, dist, arriving):
        slot = dist - 1 + (0 if dr > 0 else 4)
        block = mod(minor0[hf] - dr * (dist if arriving else dist - 1), RING)
        ref = buf.at[hf, major0[hf], block]
        to = ctx_of(hf, major0[hf], mod(minor0[hf] + dr, RING))
        return pltpu.make_async_remote_copy(
            src_ref=ref, dst_ref=ref, send_sem=ss.at[hf, slot], recv_sem=rs.at[hf, slot],
            device_id=(to, head), device_id_type=MESH,
        )

    def second(buf, ss, rs, hf, dr, item, arriving):
        dist = item // 2 + 1
        sub = jnp.where(item == 6, 0 if dr > 0 else 1, item % 2)
        major = mod(major0[hf] - dr * (dist if arriving else dist - 1), RING)
        ref = buf.at[hf, major, pl.ds(sub * 4, 4)]
        to = ctx_of(hf, mod(major0[hf] + dr, RING), minor0[hf])
        way = 0 if dr > 0 else 1
        return pltpu.make_async_remote_copy(
            src_ref=ref, dst_ref=ref, send_sem=ss.at[hf, way, item], recv_sem=rs.at[hf, way, item],
            device_id=(to, head), device_id_type=MESH,
        )

    STREAMS = [(hf, dr) for hf in (0, 1) for dr in (1, -1)]
    reach = {(0, 1): 4, (0, -1): 3, (1, 1): 3, (1, -1): 4}

    kv1 = functools.partial(first, kv, kv1_s, kv1_r)
    kv2 = functools.partial(second, kv, kv2_s, kv2_r)
    w1 = functools.partial(first, w, w1_s, w1_r)
    w2 = functools.partial(second, w, w2_s, w2_r)

    for hf, dr in STREAMS:
        kv1(hf, dr, 1, False).start()

    def weigh(a, s, v, fresh):
        n = s.shape[1]
        top = jnp.broadcast_to(jnp.max(s, axis=1, keepdims=True) * SCALE, (TOK, ADH))
        new = top if fresh else jnp.maximum(peak[a], top)
        p = jnp.exp2(s * SCALE - jnp.concatenate([new] * (n // ADH), axis=1)).astype(BF)
        pv = dot(p, jnp.concatenate([v, jnp.ones((n, ADH), BF)], axis=1))
        if fresh:
            acc[a] = pv
        else:
            shrink = jnp.exp2(peak[a] - new)
            acc[a] = acc[a] * jnp.concatenate([shrink, shrink], axis=1) + pv
        peak[a] = new

    rows = lax.broadcasted_iota(jnp.int32, (TOK, TOK), 0)
    cols = lax.broadcasted_iota(jnp.int32, (TOK, TOK), 1)
    causal = rows >= cols
    for a in range(SHARE):
        weigh(a, jnp.where(causal, dot_nt(q4[a], k_ref[...]), NEG), v_ref[...], True)

    for dist in range(1, 5):
        for hf, dr in STREAMS:
            if dist <= reach[hf, dr]:
                kv1(hf, dr, dist, True).wait_recv()
                if dist < reach[hf, dr]:
                    kv1(hf, dr, dist + 1, False).start()
    for item in (0, 1):
        for hf, dr in STREAMS:
            kv2(hf, dr, item, False).start()

    lane = lax.broadcasted_iota(jnp.int32, (1, ADH), 1) < 64

    def tri():
        return jnp.where(causal, 1.0, 0.0).astype(F32)

    def spread(pair):
        rows2 = [jnp.broadcast_to(decay_ref[pl.ds(2 * pair + i, 1), :], (64, TOK)) for i in (0, 1)]
        return dot_nt(tri(), jnp.concatenate(rows2, axis=0), lax.Precision.HIGHEST)

    def pair_columns(pair):
        return pl.ds(pl.multiple_of(pair * ADH, ADH), ADH)

    def split(vec):
        hi = vec.astype(BF)
        lo = (vec - hi.astype(F32)).astype(BF)
        return jnp.concatenate([jnp.broadcast_to(hi, (8, ADH)), jnp.broadcast_to(lo, (8, ADH))], axis=0)

    def joined(block):
        return block[64:65].astype(F32) + block[72:73].astype(F32)

    def row_copy(out, into, ss, rs, dz, arriving):
        there = mod(z + dz, RING)
        src = mod(z - dz, RING) if arriving else z
        return pltpu.make_async_remote_copy(
            src_ref=out.at[there], dst_ref=into.at[src], send_sem=ss.at[dz], recv_sem=rs.at[dz],
            device_id=(y * RING + there, head), device_id_type=MESH,
        )

    def column_copy(dy, arriving):
        there = mod(y + dy, RING)
        src = mod(y - dy, RING) if arriving else y
        return pltpu.make_async_remote_copy(
            src_ref=tot_out, dst_ref=tot_in.at[src], send_sem=tot_s.at[dy], recv_sem=tot_r.at[dy],
            device_id=(there * RING + z, head), device_id_type=MESH,
        )

    def every(f):
        def one(i, _):
            f(i)
            return 0

        lax.fori_loop(1, RING, one, 0)

    def states_out():
        arow[...] = dot_nt(decay_ref[...], tri(), lax.Precision.HIGHEST)
        bt = b_ref[...].astype(F32).T

        def one(pair, _):
            xp = x_ref[:, pair_columns(pair)]
            parts = []
            for i in (0, 1):
                a = arow[pl.ds(2 * pair + i, 1), :]
                tail = jnp.exp(a - a[:, TOK - 1 :]) * step_ref[pl.ds(2 * pair + i, 1), :]
                parts.append(dot((bt * tail).astype(BF), xp))
            state = jnp.where(lane, parts[0], parts[1]).astype(BF)
            last = [arow[pl.ds(2 * pair + i, 1), :][:, TOK - 1 :] for i in (0, 1)]
            through = split(jnp.exp(-jnp.where(lane, last[0], last[1])))
            for i in (0, 1):
                st_out[2 * pair + i, :64] = state[64 * i : 64 * i + 64]
                st_out[2 * pair + i, 64:] = through
            return 0

        lax.fori_loop(0, 4, one, 0)
        every(lambda dz: row_copy(st_out, st_in, st_s, st_r, dz, False).start())
        st_in[z] = st_out[z]

    def totals_out():
        every(lambda dz: row_copy(st_out, st_in, st_s, st_r, dz, True).wait_recv())

        def one(i, carry):
            state, decay = carry
            pre[i] = state
            predec[i] = jnp.broadcast_to(decay, (8, ADH))
            block = st_in[i]
            t = joined(block)
            return t * state + block[:64].astype(F32), t * decay

        state, decay = lax.fori_loop(0, RING, one, (jnp.zeros((64, ADH), F32), jnp.ones((1, ADH), F32)))
        tot_out[:64] = state.astype(BF)
        tot_out[64:] = split(decay)
        every(lambda dy: column_copy(dy, False).start())

    def incoming_out():
        every(lambda dy: column_copy(dy, True).wait_recv())

        def one(i, state):
            block = tot_in[i]
            return joined(block) * state + block[:64].astype(F32)

        state = lax.fori_loop(0, y, one, jnp.zeros((64, ADH), F32))

        def give(i, _):
            ret_out[i] = (pre[i] + predec[i][:1] * state).astype(BF)
            return 0

        lax.fori_loop(0, RING, give, 0)
        every(lambda dz: row_copy(ret_out, ret_in, ret_s, ret_r, dz, False).start())
        ret_in[z] = ret_out[z]

    def mix():
        every(lambda dz: row_copy(ret_out, ret_in, ret_s, ret_r, dz, True).wait_recv())
        scores[...] = dot_nt(c_ref[...], b_ref[...])

        def one(pair, squares):
            at = pair_columns(pair)
            xp = x_ref[:, at]
            a_t = spread(pair)
            parts = []
            for i in (0, 1):
                a_u = arow[pl.ds(2 * pair + i, 1), :]
                gap = jnp.where(causal, a_u - a_t[:, 64 * i : 64 * i + 1], NEG)
                mixing = jnp.exp(gap) * (scores[...] * step_ref[pl.ds(2 * pair + i, 1), :])
                parts.append(dot(mixing.astype(BF), xp))
            carried = dot(c_ref[...], ret_in[pl.ds(2 * pair, 2)].reshape(ADH, ADH)) * jnp.exp(-a_t)
            skip = jnp.where(lane, skip_ref[2 * pair], skip_ref[2 * pair + 1])
            total = jnp.where(lane, parts[0], parts[1]) + carried + skip * xp.astype(F32)
            g = gate_ref[:, at].astype(F32)
            total = total * (g / (1.0 + jnp.exp(-g)))
            gated[:, at] = total
            return squares + jnp.sum(total * total, axis=1, keepdims=True)

        squares = lax.fori_loop(0, 4, one, jnp.zeros((TOK, 1), F32))
        norm = lax.rsqrt(squares / 512.0 + 1e-05)
        ssm_ref[...] = (gated[...] * norm * gain_ref[...].astype(F32)).astype(BF)

    def attend(step):
        def one(st, _):
            hf = st // 2
            late = st % 2
            dist = (step + 1) // 2
            dr = 1 - 2 * late
            base = jnp.where(hf == 0, y, z)
            major = mod(base - dr * dist, RING)
            sub = jnp.where((step == 0) | (step == 7), late, (step + 1) % 2)
            stride = jnp.where(hf == 0, 1, RING)
            u0 = jnp.where(hf == 0, major * RING + sub * 4, sub * 4 * RING + major)

            @pl.when(u0 < me)
            def _():
                keys = kv[hf, major, pl.ds(sub * 4, 4), 0].reshape(4 * HALF, ADH)
                values = kv[hf, major, pl.ds(sub * 4, 4), 1].reshape(4 * HALF, ADH)
                block = lax.broadcasted_iota(jnp.int32, (1, 4 * HALF), 1) // HALF
                bias = jnp.where(u0 + block * stride < me, 0.0, NEG)
                for a in range(SHARE):
                    weigh(a, dot_nt(q4[a], keys) + bias, values, False)

            return 0

        lax.fori_loop(0, 4, one, 0)

    def pass_on(copy, item):
        for hf, dr in STREAMS:
            copy(hf, dr, item, True).wait_recv()

            @pl.when(item < (5 if dr > 0 else 4))
            def _(hf=hf, dr=dr):
                copy(hf, dr, jnp.minimum(item + 2, 6), False).start()

            if dr < 0:

                @pl.when(item == 5)
                def _(hf=hf, dr=dr):
                    copy(hf, dr, 6, False).start()

    def step(i, _):
        @pl.when(i >= 1)
        def _():
            pass_on(kv2, i - 1)

        for hf, dr in STREAMS:
            far = reach[hf, dr]

            @pl.when((i >= 1) & (i <= far))
            def _(hf=hf, dr=dr):
                w1(hf, dr, jnp.maximum(i, 1), True).wait_recv()

            @pl.when(i < far)
            def _(hf=hf, dr=dr):
                w1(hf, dr, i + 1, False).start()

        @pl.when(i == 6)
        def _():
            for item in (0, 1):
                for hf, dr in STREAMS:
                    w2(hf, dr, item, False).start()

        pl.when(i == 0)(states_out)
        pl.when(i == 1)(totals_out)
        pl.when(i == 2)(incoming_out)
        pl.when(i == 3)(mix)
        attend(i)
        return 0

    lax.fori_loop(0, 8, step, 0)

    for a in range(SHARE):
        heads[:, a * ADH : (a + 1) * ADH] = (acc[a][:, :ADH] / acc[a][:, ADH:]).astype(BF)

    def w_step(i, _):
        pass_on(w2, i)
        return 0

    lax.fori_loop(0, 7, w_step, 0)

    def product(f):
        left = dot_nt(heads[:, :256], w[0, f].reshape(512, 256))
        right = dot_nt(heads[:, 256:], w[1, :, f].reshape(512, 256))
        return (left + right).astype(BF)

    def sib_copy(o):
        return pltpu.make_async_remote_copy(
            src_ref=sib_out.at[o], dst_ref=sib_in.at[o], send_sem=sib_s.at[o], recv_sem=sib_r.at[o],
            device_id=(me, 2 * xc + 1 - core), device_id_type=MESH,
        )

    def side(way):
        return (me, 2 * mod(xc + (1 if way == 0 else -1), XS) + core)

    def x1_copy(way):
        return pltpu.make_async_remote_copy(
            src_ref=x1_out.at[way], dst_ref=x1_in.at[way], send_sem=x1_s.at[way], recv_sem=x1_r.at[way],
            device_id=side(way), device_id_type=MESH,
        )

    def x2_copy(way):
        return pltpu.make_async_remote_copy(
            src_ref=x2_out.at[way], dst_ref=x2_in.at[way], send_sem=x2_s.at[way], recv_sem=x2_r.at[way],
            device_id=side(way), device_id_type=MESH,
        )

    for o in (2, 1, 3, 0):
        chip = mod(xc + o, XS)
        sib_out[o] = product(2 * chip + 1 - core)
        sib_copy(o).start()
        mine[o] = product(2 * chip + core)

    def both(o, lo, hi):
        return mine[o, lo:hi].astype(F32) + sib_in[o, lo:hi].astype(F32)

    sib_copy(2).wait_recv()
    x1_out[0] = both(2, 0, HALF).astype(BF)
    x1_copy(0).start()
    x1_out[1] = both(2, HALF, TOK).astype(BF)
    x1_copy(1).start()
    sib_copy(1).wait_recv()
    x2_out[0, HALF:] = both(1, HALF, TOK).astype(BF)
    x1_copy(0).wait_recv()
    x2_out[0, :HALF] = (both(1, 0, HALF) + x1_in[0].astype(F32)).astype(BF)
    x2_copy(0).start()
    sib_copy(3).wait_recv()
    x2_out[1, :HALF] = both(3, 0, HALF).astype(BF)
    x1_copy(1).wait_recv()
    x2_out[1, HALF:] = (both(3, HALF, TOK) + x1_in[1].astype(F32)).astype(BF)
    x2_copy(1).start()
    sib_copy(0).wait_recv()
    x2_copy(0).wait_recv()
    x2_copy(1).wait_recv()
    out_ref[...] = (both(0, 0, TOK) + x2_in[0].astype(F32) + x2_in[1].astype(F32)).astype(BF)

    for hf, dr in STREAMS:
        for dist in range(1, reach[hf, dr] + 1):
            kv1(hf, dr, dist, False).wait_send()
            w1(hf, dr, dist, False).wait_send()

        def sent(item, _, hf=hf, dr=dr):
            kv2(hf, dr, item, False).wait_send()
            w2(hf, dr, item, False).wait_send()
            return 0

        lax.fori_loop(0, 7, sent, 0)
    every(lambda d: row_copy(st_out, st_in, st_s, st_r, d, False).wait_send())
    every(lambda d: column_copy(d, False).wait_send())
    every(lambda d: row_copy(ret_out, ret_in, ret_s, ret_r, d, False).wait_send())
    for o in range(4):
        sib_copy(o).wait_send()
    for way in (0, 1):
        x1_copy(way).wait_send()
        x2_copy(way).wait_send()


def per_device(
    x_in, gate_z, b_in, c_in, step_size, log_decay, d_skip, norm_gain, query, key, value, o_weight
):
    vmem = pl.BlockSpec(memory_space=pltpu.VMEM)
    smem = pl.BlockSpec(memory_space=pltpu.SMEM)
    dma = pltpu.SemaphoreType.DMA
    tokens = (TOK, 512)
    return pl.pallas_call(
        kernel,
        out_shape=(jax.ShapeDtypeStruct(tokens, BF), jax.ShapeDtypeStruct(tokens, BF)),
        in_specs=[vmem] * 6 + [smem] + [vmem] * 5,
        out_specs=(vmem, vmem),
        scratch_shapes=[
            pltpu.VMEM((2, RING, RING, 2, HALF, ADH), BF),
            pltpu.VMEM((2, RING, RING, 64, 256), BF),
            pltpu.VMEM((SHARE, TOK, ADH), BF),
            pltpu.VMEM((SHARE, TOK, 2 * ADH), F32),
            pltpu.VMEM((SHARE, TOK, ADH), F32),
            pltpu.VMEM(tokens, BF),
            pltpu.VMEM((8, TOK), F32),
            pltpu.VMEM((TOK, TOK), F32),
            pltpu.VMEM(tokens, F32),
            pltpu.VMEM((RING, 80, ADH), BF),
            pltpu.VMEM((RING, 80, ADH), BF),
            pltpu.VMEM((RING, 64, ADH), F32),
            pltpu.VMEM((RING, 8, ADH), F32),
            pltpu.VMEM((80, ADH), BF),
            pltpu.VMEM((RING, 80, ADH), BF),
            pltpu.VMEM((RING, 64, ADH), BF),
            pltpu.VMEM((RING, 64, ADH), BF),
            pltpu.VMEM((XS,) + tokens, BF),
            pltpu.VMEM((XS,) + tokens, BF),
            pltpu.VMEM((XS,) + tokens, BF),
            pltpu.VMEM((2, HALF, 512), BF),
            pltpu.VMEM((2, HALF, 512), BF),
            pltpu.VMEM((2,) + tokens, BF),
            pltpu.VMEM((2,) + tokens, BF),
            dma((2, 8)), dma((2, 8)), dma((2, 2, 7)), dma((2, 2, 7)),
            dma((2, 8)), dma((2, 8)), dma((2, 2, 7)), dma((2, 2, 7)),
            dma((8,)), dma((8,)), dma((8,)), dma((8,)), dma((8,)), dma((8,)),
            dma((4,)), dma((4,)), dma((2,)), dma((2,)), dma((2,)), dma((2,)),
        ],
        compiler_params=pltpu.CompilerParams(
            collective_id=0, has_side_effects=True, vmem_limit_bytes=48 * 1024 * 1024
        ),
        name="mixer_and_attention",
    )(
        x_in, gate_z, b_in, c_in, step_size, log_decay, d_skip, norm_gain.reshape(1, 512),
        query, key, value, o_weight.T,
    )


def solution(mesh):
    in_specs = (
        P("ctx", "head"),
        P("ctx", "head"),
        P("ctx", "head"),
        P("ctx", "head"),
        P("head", "ctx"),
        P("head", "ctx"),
        P("head"),
        P("head"),
        P("ctx", "head"),
        P("ctx", "head"),
        P("ctx", "head"),
        P("head", "ctx"),
    )
    out_specs = (P("ctx", "head"), P("ctx", "head"))
    return jax.shard_map(
        per_device, mesh=mesh, in_specs=in_specs, out_specs=out_specs, check_vma=False
    )
```

```python
import functools
import math

import jax
import jax.numpy as jnp
from jax import lax
from jax.experimental import pallas as pl
from jax.experimental.pallas import tpu as pltpu
from jax.sharding import PartitionSpec as P

MESH = pl.DeviceIdType.MESH
BF = jnp.bfloat16
F32 = jnp.float32
TOK = 256
HALF = TOK // 2
ADH = 128
SHARE = 4
RING = 8
XS = 4
NEG = -1e30
SCALE = math.log2(math.e) / math.sqrt(ADH)
NT = (((1,), (1,)), ((), ()))


def mod(a, n):
    return lax.rem(a + 2 * n, n)


def dot(a, b):
    return jnp.dot(a, b, preferred_element_type=F32)


def dot_nt(a, b, precision=None):
    return lax.dot_general(a, b, NT, precision=precision, preferred_element_type=F32)


def kernel(
    x_hbm, gate_hbm, b_hbm, c_hbm, step_hbm, decay_hbm, skip_ref, gain_ref, q_hbm, k_hbm, v_hbm, wt_hbm,
    ssm_ref, out_ref,
    x_ref, gate_ref, b_ref, c_ref, step_ref, decay_ref,
    kv, qs, w, acc, peak, part_o, part_l, tx_o, tx_l, rx_o, rx_l, heads,
    arow, scores, gated, squares, st_out, st_in, pre, predec, tot_out, tot_in, ret_out, ret_in,
    sib_out, sib_in, mine, x1_out, x1_in, x2_out, x2_in,
    in_s, skv_s, skv_r, sq_s, sq_r, sw_s, sw_r, kr_s, kr_r, qr_s, qr_r, o_s, o_r, l_s, l_r,
    w1_s, w1_r, w2_s, w2_r,
    st_s, st_r, tot_s, tot_r, ret_s, ret_r, sib_s, sib_r, x1_s, x1_r, x2_s, x2_r,
):
    me = lax.axis_index("ctx")
    head = lax.axis_index("head")
    y, z = me // RING, me % RING
    xc, core = head // 2, head % 2
    sibling = (me, 2 * xc + 1 - core)
    major0, minor0 = (y, z), (z, y)

    def q_place(m):
        return jnp.where(m == 0, z, y)

    def k_place(m):
        return jnp.where(m == 0, y, z)

    def ctx_at(m, q, k):
        return jnp.where(m == 0, k * RING + q, q * RING + k)

    def ctx_of(hf, major, minor):
        return major * RING + minor if hf == 0 else minor * RING + major

    barrier = pltpu.get_barrier_semaphore()

    def greet(i, _):
        pl.semaphore_signal(barrier, inc=1, device_id=(y * RING + mod(z + i, RING), head), device_id_type=MESH)
        pl.semaphore_signal(barrier, inc=1, device_id=(mod(y + i, RING) * RING + z, head), device_id_type=MESH)
        pl.semaphore_signal(barrier, inc=1, device_id=(me, mod(head + i, 8)), device_id_type=MESH)
        return 0

    lax.fori_loop(1, 8, greet, 0)

    my_k, my_q = k_place(core), q_place(core)

    def lanes(block, width):
        return pl.ds(pl.multiple_of(block * width, width), width)

    fetches = [
        (k_hbm, kv.at[core, my_k, 0]),
        (v_hbm, kv.at[core, my_k, 1]),
        (q_hbm.at[:, lanes(2 * core, ADH)], qs.at[core, my_q, 0]),
        (q_hbm.at[:, lanes(2 * core + 1, ADH)], qs.at[core, my_q, 1]),
        (wt_hbm.at[:, lanes(core, 256)], w.at[core, my_k, my_q]),
        (decay_hbm, decay_ref),
        (b_hbm, b_ref),
        (x_hbm, x_ref),
        (step_hbm, step_ref),
        (c_hbm, c_ref),
        (gate_hbm, gate_ref),
    ]
    fetches = [pltpu.make_async_copy(src, dst, in_s.at[i]) for i, (src, dst) in enumerate(fetches)]
    for fetch in fetches:
        fetch.start()
    for fetch in fetches[:2]:
        fetch.wait()
    pl.semaphore_wait(barrier, 21)

    def sib_kv(m, place):
        ref = kv.at[m, place]
        return pltpu.make_async_remote_copy(
            src_ref=ref, dst_ref=ref, send_sem=skv_s.at[place], recv_sem=skv_r.at[place],
            device_id=sibling, device_id_type=MESH,
        )

    def sib_q(m, i):
        return pltpu.make_async_remote_copy(
            src_ref=q_hbm.at[:, lanes(2 * (1 - core) + i, ADH)], dst_ref=qs.at[m, q_place(m), i],
            send_sem=sq_s.at[i], recv_sem=sq_r.at[i], device_id=sibling, device_id_type=MESH,
        )

    def sib_w(m):
        return pltpu.make_async_remote_copy(
            src_ref=wt_hbm.at[:, lanes(1 - core, 256)], dst_ref=w.at[m, k_place(m), q_place(m)],
            send_sem=sw_s, recv_sem=sw_r, device_id=sibling, device_id_type=MESH,
        )

    def ring_kv(dr, dist, arriving):
        way = 0 if dr > 0 else 1
        place = mod(my_k - dr * (dist if arriving else dist - 1), RING)
        ref = kv.at[core, place] if dist < 4 else kv.at[core, place, way]
        to = ctx_at(core, my_q, mod(my_k + dr, RING))
        return pltpu.make_async_remote_copy(
            src_ref=ref, dst_ref=ref, send_sem=kr_s.at[way, dist - 1], recv_sem=kr_r.at[way, dist - 1],
            device_id=(to, head), device_id_type=MESH,
        )

    def ring_q(m, dr, dist, arriving):
        way = 0 if dr > 0 else 1
        place = mod(q_place(m) - dr * (dist if arriving else dist - 1), RING)
        ref = qs.at[m, place] if dist < 4 else qs.at[m, place, way]
        to = ctx_at(m, mod(q_place(m) + dr, RING), k_place(m))
        return pltpu.make_async_remote_copy(
            src_ref=ref, dst_ref=ref, send_sem=qr_s.at[m, way, dist - 1], recv_sem=qr_r.at[m, way, dist - 1],
            device_id=(to, head), device_id_type=MESH,
        )

    def kv_hop(dist):
        for dr in (1, -1):
            ring_kv(dr, dist, True).wait_recv()
            if dist < 4:
                ring_kv(dr, dist + 1, False).start()
                sib_kv(core, mod(my_k - dr * dist, RING)).start()
        if dist == 4:
            sib_kv(core, mod(my_k + 4, RING)).start()

    def q_hop(dist):
        for m in (0, 1):
            for dr in (1, -1):
                if dist > 0:
                    ring_q(m, dr, dist, True).wait_recv()
                if dist < 4:
                    ring_q(m, dr, dist + 1, False).start()

    def first(buf, ss, rs, hf, dr, dist, arriving):
        slot = dist - 1 + (0 if dr > 0 else 4)
        block = mod(minor0[hf] - dr * (dist if arriving else dist - 1), RING)
        ref = buf.at[hf, major0[hf], block]
        to = ctx_of(hf, major0[hf], mod(minor0[hf] + dr, RING))
        return pltpu.make_async_remote_copy(
            src_ref=ref, dst_ref=ref, send_sem=ss.at[hf, slot], recv_sem=rs.at[hf, slot],
            device_id=(to, head), device_id_type=MESH,
        )

    def second(buf, ss, rs, hf, dr, item, arriving):
        dist = item // 2 + 1
        sub = (0 if dr > 0 else 1) if item == 6 else item % 2
        major = mod(major0[hf] - dr * (dist if arriving else dist - 1), RING)
        ref = buf.at[hf, major, sub * 4 : sub * 4 + 4]
        to = ctx_of(hf, mod(major0[hf] + dr, RING), minor0[hf])
        way = 0 if dr > 0 else 1
        return pltpu.make_async_remote_copy(
            src_ref=ref, dst_ref=ref, send_sem=ss.at[hf, way, item], recv_sem=rs.at[hf, way, item],
            device_id=(to, head), device_id_type=MESH,
        )

    STREAMS = [(hf, dr) for hf in (0, 1) for dr in (1, -1)]
    reach = {(0, 1): 4, (0, -1): 3, (1, 1): 3, (1, -1): 4}
    w1 = functools.partial(first, w, w1_s, w1_r)
    w2 = functools.partial(second, w, w2_s, w2_r)

    def w_hop(dist):
        for hf, dr in STREAMS:
            if 0 < dist <= reach[hf, dr]:
                w1(hf, dr, dist, True).wait_recv()
            if dist < reach[hf, dr]:
                w1(hf, dr, dist + 1, False).start()

    def w_pass(item):
        for hf, dr in STREAMS:
            w2(hf, dr, item, True).wait_recv()
            if item < (5 if dr > 0 else 4):
                w2(hf, dr, min(item + 2, 6), False).start()
            elif dr < 0 and item == 5:
                w2(hf, dr, 6, False).start()

    def w_rows():
        for item in (0, 1):
            for hf, dr in STREAMS:
                w2(hf, dr, item, False).start()

    sib_kv(core, my_k).start()
    for i in (0, 1):
        sib_q(core, i).start()
    for dr in (1, -1):
        ring_kv(dr, 1, False).start()
    sib_w(core).start()
    for fetch in fetches[2:]:
        fetch.wait()

    def weigh(m, i, s, v, fresh):
        n = s.shape[1]
        top = jnp.broadcast_to(jnp.max(s, axis=1, keepdims=True) * SCALE, (TOK, ADH))
        new = top if fresh else jnp.maximum(peak[m, i], top)
        p = jnp.exp2(s * SCALE - jnp.concatenate([new] * (n // ADH), axis=1)).astype(BF)
        pv = dot(p, jnp.concatenate([v, jnp.ones((n, ADH), BF)], axis=1))
        if fresh:
            acc[m, i] = pv
        else:
            shrink = jnp.exp2(peak[m, i] - new)
            acc[m, i] = acc[m, i] * jnp.concatenate([shrink, shrink], axis=1) + pv
        peak[m, i] = new

    rows = lax.broadcasted_iota(jnp.int32, (TOK, TOK), 0)
    cols = lax.broadcasted_iota(jnp.int32, (TOK, TOK), 1)
    causal = rows >= cols

    def own_block(m, _):
        at, q = k_place(m), q_place(m)
        for i in (0, 1):
            s = jnp.where(causal, dot_nt(qs[m, q, i], kv[m, at, 0]), NEG)
            weigh(m, i, s, kv[m, at, 1], True)
        return 0

    def tile(step):
        away = jnp.where(step == 1, 1, jnp.where(step == 2, 7, jnp.where(step == 3, 2, jnp.where(step == 4, 6, 0))))
        away = jnp.where(step == 5, 4, jnp.where(step == 6, 3, jnp.where(step == 7, 5, away)))

        def one(m, _):
            q = mod(q_place(m) + away, RING)
            at_z = y + jnp.where(q > z, 1, 0)
            at_y = jnp.where(q > y, RING, jnp.where(q == y, z, 0))
            blocks = jnp.where(m == 0, at_z, at_y)

            @pl.when(step > 0)
            def _():
                acc[m] = jnp.zeros((2, TOK, 2 * ADH), F32)
                peak[m] = jnp.full((2, TOK, ADH), NEG, F32)

            def keys(t, _):
                ks = kv[m, pl.ds(2 * t, 2), 0].reshape(2 * TOK, ADH)
                vs = kv[m, pl.ds(2 * t, 2), 1].reshape(2 * TOK, ADH)
                block = 2 * t + lax.broadcasted_iota(jnp.int32, (1, 2 * TOK), 1) // TOK
                bias = jnp.where(block < blocks, 0.0, NEG)
                for i in (0, 1):
                    weigh(m, i, dot_nt(qs[m, q, i], ks) + bias, vs, False)
                return 0

            lax.fori_loop(0, (blocks + 1) // 2, keys, 0)
            for i in (0, 1):
                total = jnp.maximum(acc[m, i][:, ADH:], 1e-30)
                part_o[m, away, i] = acc[m, i][:, :ADH] / total
                part_l[m, away, i] = peak[m, i] + jnp.log2(total)
            return 0

        lax.fori_loop(0, 2, one, 0)

    small = lax.broadcasted_iota(jnp.int32, (ADH, ADH), 0) == lax.broadcasted_iota(jnp.int32, (ADH, ADH), 1)

    def packed(l):
        halves = [l[r * ADH : (r + 1) * ADH] for r in (0, 1)]
        return [jnp.sum(jnp.where(small, half, 0.0), axis=0, keepdims=True) for half in halves]

    def unpacked(block, i):
        halves = []
        for r in (0, 1):
            row = jnp.broadcast_to(block[2 * i + r : 2 * i + r + 1], (ADH, ADH))
            column = jnp.sum(jnp.where(small, row, 0.0), axis=1, keepdims=True)
            halves.append(jnp.broadcast_to(column, (ADH, ADH)))
        return jnp.concatenate(halves, axis=0)

    def join(o1, l1, o2, l2):
        top = jnp.maximum(l1, l2)
        w1_, w2_ = jnp.exp2(l1 - top), jnp.exp2(l2 - top)
        total = w1_ + w2_
        return (o1 * w1_ + o2 * w2_) / total, top + jnp.log2(total)

    def back_o(m, way, k):
        at = (m, way, k - 1) if k < 4 else (m, way, 3, way)
        to = ctx_at(m, mod(q_place(m) + (1 if way == 0 else -1), RING), k_place(m))
        return pltpu.make_async_remote_copy(
            src_ref=tx_o.at[at], dst_ref=rx_o.at[at], send_sem=o_s.at[m, way, k - 1], recv_sem=o_r.at[m, way, k - 1],
            device_id=(to, head), device_id_type=MESH,
        )

    def back_l(m, way, k):
        at = (m, way, k - 1)
        to = ctx_at(m, mod(q_place(m) + (1 if way == 0 else -1), RING), k_place(m))
        return pltpu.make_async_remote_copy(
            src_ref=tx_l.at[at], dst_ref=rx_l.at[at], send_sem=l_s.at[at], recv_sem=l_r.at[at],
            device_id=(to, head), device_id_type=MESH,
        )

    def back(k, way):
        away = k if way == 0 else RING - k

        def one(m, _):
            if k < 4:
                back_o(m, way, k + 1).wait_recv()
                back_l(m, way, k + 1).wait_recv()
            stats = []
            for i in (0, 1):
                o, l = part_o[m, away, i], part_l[m, away, i]
                if k < 3 or (k == 3 and i == way):
                    came = rx_o[m, way, k, i].astype(F32)
                    o, l = join(o, l, came, unpacked(rx_l[m, way, k], i))
                if k < 4 or i == way:
                    tx_o[m, way, k - 1, i] = o.astype(BF)
                stats += packed(l)
            tx_l[m, way, k - 1] = jnp.concatenate(stats + [jnp.zeros((4, ADH), F32)], axis=0)
            back_o(m, way, k).start()
            back_l(m, way, k).start()
            return 0

        lax.fori_loop(0, 2, one, 0)

    def collect():
        for m in (0, 1):
            for way in (0, 1):
                back_o(m, way, 1).wait_recv()
                back_l(m, way, 1).wait_recv()
            for i in (0, 1):
                o, l = part_o[m, 0, i], part_l[m, 0, i]
                for way in (0, 1):
                    came = rx_o[m, way, 0, i].astype(F32)
                    o, l = join(o, l, came, unpacked(rx_l[m, way, 0], i))
                f = 2 * m + i
                heads[:, f * ADH : (f + 1) * ADH] = o.astype(BF)

    lane = lax.broadcasted_iota(jnp.int32, (1, ADH), 1) < 64

    def tri():
        return jnp.where(causal, 1.0, 0.0).astype(F32)

    def spread(pair):
        rows2 = [jnp.broadcast_to(decay_ref[pl.ds(2 * pair + i, 1), :], (64, TOK)) for i in (0, 1)]
        return dot_nt(tri(), jnp.concatenate(rows2, axis=0), lax.Precision.HIGHEST)

    def pair_columns(pair):
        return lanes(pair, ADH)

    def split(vec):
        hi = vec.astype(BF)
        lo = (vec - hi.astype(F32)).astype(BF)
        return jnp.concatenate([jnp.broadcast_to(hi, (8, ADH)), jnp.broadcast_to(lo, (8, ADH))], axis=0)

    def joined(block):
        return block[64:65].astype(F32) + block[72:73].astype(F32)

    def row_copy(out, into, ss, rs, dz, arriving):
        there = mod(z + dz, RING)
        src = mod(z - dz, RING) if arriving else z
        return pltpu.make_async_remote_copy(
            src_ref=out.at[there], dst_ref=into.at[src], send_sem=ss.at[dz], recv_sem=rs.at[dz],
            device_id=(y * RING + there, head), device_id_type=MESH,
        )

    def column_copy(dy, arriving):
        there = mod(y + dy, RING)
        src = mod(y - dy, RING) if arriving else y
        return pltpu.make_async_remote_copy(
            src_ref=tot_out, dst_ref=tot_in.at[src], send_sem=tot_s.at[dy], recv_sem=tot_r.at[dy],
            device_id=(there * RING + z, head), device_id_type=MESH,
        )

    def every(f):
        def one(i, _):
            f(i)
            return 0

        lax.fori_loop(1, RING, one, 0)

    def states_out():
        arow[...] = dot_nt(decay_ref[...], tri(), lax.Precision.HIGHEST)
        bt = b_ref[...].astype(F32).T

        def one(pair, _):
            xp = x_ref[:, pair_columns(pair)]
            parts = []
            for i in (0, 1):
                a = arow[pl.ds(2 * pair + i, 1), :]
                tail = jnp.exp(a - a[:, TOK - 1 :]) * step_ref[pl.ds(2 * pair + i, 1), :]
                parts.append(dot((bt * tail).astype(BF), xp))
            state = jnp.where(lane, parts[0], parts[1]).astype(BF)
            last = [arow[pl.ds(2 * pair + i, 1), :][:, TOK - 1 :] for i in (0, 1)]
            through = split(jnp.exp(-jnp.where(lane, last[0], last[1])))
            for i in (0, 1):
                st_out[2 * pair + i, :64] = state[64 * i : 64 * i + 64]
                st_out[2 * pair + i, 64:] = through
            return 0

        lax.fori_loop(0, 4, one, 0)
        every(lambda dz: row_copy(st_out, st_in, st_s, st_r, dz, False).start())
        st_in[z] = st_out[z]

    def totals_out():
        every(lambda dz: row_copy(st_out, st_in, st_s, st_r, dz, True).wait_recv())

        def one(i, carry):
            state, decay = carry
            pre[i] = state
            predec[i] = jnp.broadcast_to(decay, (8, ADH))
            block = st_in[i]
            t = joined(block)
            return t * state + block[:64].astype(F32), t * decay

        state, decay = lax.fori_loop(0, RING, one, (jnp.zeros((64, ADH), F32), jnp.ones((1, ADH), F32)))
        tot_out[:64] = state.astype(BF)
        tot_out[64:] = split(decay)
        every(lambda dy: column_copy(dy, False).start())

    def incoming_out():
        every(lambda dy: column_copy(dy, True).wait_recv())

        def one(i, state):
            block = tot_in[i]
            return joined(block) * state + block[:64].astype(F32)

        state = lax.fori_loop(0, y, one, jnp.zeros((64, ADH), F32))

        def give(i, _):
            ret_out[i] = (pre[i] + predec[i][:1] * state).astype(BF)
            return 0

        lax.fori_loop(0, RING, give, 0)
        every(lambda dz: row_copy(ret_out, ret_in, ret_s, ret_r, dz, False).start())
        ret_in[z] = ret_out[z]

    def mix_pair(pair):
        if pair == 0:
            every(lambda dz: row_copy(ret_out, ret_in, ret_s, ret_r, dz, True).wait_recv())
            scores[...] = dot_nt(c_ref[...], b_ref[...])
            squares[...] = jnp.zeros_like(squares)

        at = pair_columns(pair)
        xp = x_ref[:, at]
        a_t = spread(pair)
        parts = []
        for i in (0, 1):
            a_u = arow[pl.ds(2 * pair + i, 1), :]
            gap = jnp.where(causal, a_u - a_t[:, 64 * i : 64 * i + 1], NEG)
            mixing = jnp.exp(gap) * (scores[...] * step_ref[pl.ds(2 * pair + i, 1), :])
            parts.append(dot(mixing.astype(BF), xp))
        carried = dot(c_ref[...], ret_in[pl.ds(2 * pair, 2)].reshape(ADH, ADH)) * jnp.exp(-a_t)
        skip = jnp.where(lane, skip_ref[2 * pair], skip_ref[2 * pair + 1])
        total = jnp.where(lane, parts[0], parts[1]) + carried + skip * xp.astype(F32)
        g = gate_ref[:, at].astype(F32)
        total = total * (g / (1.0 + jnp.exp(-g)))
        gated[:, at] = total
        squares[...] += jnp.broadcast_to(jnp.sum(total * total, axis=1, keepdims=True), (TOK, ADH))

    def mix_end():
        norm = lax.rsqrt(squares[...] / 512.0 + 1e-05)
        norm = jnp.concatenate([norm] * 4, axis=1)
        ssm_ref[...] = (gated[...] * norm * gain_ref[...].astype(F32)).astype(BF)

    sib_w(1 - core).wait_recv()
    w_hop(0)
    for i in (0, 1):
        sib_q(1 - core, i).wait_recv()
    kv_hop(1)
    states_out()
    kv_hop(2)
    q_hop(0)
    sib_kv(1 - core, k_place(1 - core)).wait_recv()
    lax.fori_loop(0, 2, own_block, 0)
    kv_hop(3)
    w_hop(1)
    kv_hop(4)
    totals_out()
    q_hop(1)
    w_hop(2)

    def rest(i, _):
        sib_kv(1 - core, mod(k_place(1 - core) + i, RING)).wait_recv()
        return 0

    lax.fori_loop(1, RING, rest, 0)

    def step(i, _):
        @pl.when(i == 1)
        def _():
            q_hop(2)
            w_hop(3)

        @pl.when(i == 2)
        def _():
            q_hop(3)
            w_hop(4)
            w_rows()

        @pl.when(i == 3)
        def _():
            q_hop(4)
            incoming_out()

        @pl.when(i == 5)
        def _():
            w_pass(0)

        tile(i)

        @pl.when(i == 5)
        def _():
            back(4, 0)
            back(4, 1)

        @pl.when(i == 6)
        def _():
            back(3, 0)
            w_pass(1)

        return 0

    lax.fori_loop(0, 8, step, 0)
    back(3, 1)
    mix_pair(0)
    w_pass(2)
    back(2, 0)
    back(2, 1)
    mix_pair(1)
    w_pass(3)
    back(1, 0)
    back(1, 1)
    mix_pair(2)
    w_pass(4)
    mix_pair(3)
    collect()
    w_pass(5)
    w_pass(6)

    def product(f):
        left = dot_nt(heads[:, :256], w[0, f].reshape(512, 256))
        right = dot_nt(heads[:, 256:], w[1, :, f].reshape(512, 256))
        return (left + right).astype(BF)

    def sib_copy(o):
        return pltpu.make_async_remote_copy(
            src_ref=sib_out.at[o], dst_ref=sib_in.at[o], send_sem=sib_s.at[o], recv_sem=sib_r.at[o],
            device_id=(me, 2 * xc + 1 - core), device_id_type=MESH,
        )

    def side(way):
        return (me, 2 * mod(xc + (1 if way == 0 else -1), XS) + core)

    def x1_copy(way):
        return pltpu.make_async_remote_copy(
            src_ref=x1_out.at[way], dst_ref=x1_in.at[way], send_sem=x1_s.at[way], recv_sem=x1_r.at[way],
            device_id=side(way), device_id_type=MESH,
        )

    def x2_copy(way, part):
        ref = (way, pl.ds(part * HALF, HALF))
        return pltpu.make_async_remote_copy(
            src_ref=x2_out.at[ref], dst_ref=x2_in.at[ref], send_sem=x2_s.at[way, part], recv_sem=x2_r.at[way, part],
            device_id=side(way), device_id_type=MESH,
        )

    def for_sibling(o):
        sib_out[o] = product(2 * mod(xc + o, XS) + 1 - core)
        sib_copy(o).start()

    def for_own(o):
        mine[o] = product(2 * mod(xc + o, XS) + core)

    def both(o, part):
        at = pl.ds(part * HALF, HALF)
        return mine[o, at].astype(F32) + sib_in[o, at].astype(F32)

    for_sibling(2)
    for_own(2)
    for_sibling(1)
    for_sibling(3)
    sib_copy(2).wait_recv()
    for way in (0, 1):
        x1_out[way] = both(2, way).astype(BF)
        x1_copy(way).start()
    for way, o in ((0, 1), (1, 3)):
        for_own(o)
        sib_copy(o).wait_recv()
        x2_out[way, (1 - way) * HALF : (2 - way) * HALF] = both(o, 1 - way).astype(BF)
        x2_copy(way, 1 - way).start()
    for way, o in ((0, 1), (1, 3)):
        x1_copy(way).wait_recv()
        x2_out[way, way * HALF : (way + 1) * HALF] = (both(o, way) + x1_in[way].astype(F32)).astype(BF)
        x2_copy(way, way).start()
    for_sibling(0)
    for_own(0)
    mix_end()
    sib_copy(0).wait_recv()
    for part in (1, 0):
        x2_copy(0, part).wait_recv()
        x2_copy(1, part).wait_recv()
    for part in (0, 1):
        at = pl.ds(part * HALF, HALF)
        out_ref[at] = (both(0, part) + x2_in[0, at].astype(F32) + x2_in[1, at].astype(F32)).astype(BF)

    def sent(i, _):
        sib_kv(core, i).wait_send()
        return 0

    lax.fori_loop(0, RING, sent, 0)
    for i in (0, 1):
        sib_q(core, i).wait_send()
    sib_w(core).wait_send()
    for dist in range(1, 5):
        for dr in (1, -1):
            ring_kv(dr, dist, False).wait_send()

    def sent_both(m, _):
        for k in range(1, 5):
            for way, dr in ((0, 1), (1, -1)):
                ring_q(m, dr, k, False).wait_send()
                back_o(m, way, k).wait_send()
                back_l(m, way, k).wait_send()
        return 0

    lax.fori_loop(0, 2, sent_both, 0)
    for hf, dr in STREAMS:
        for dist in range(1, reach[hf, dr] + 1):
            w1(hf, dr, dist, False).wait_send()
        for item in range(7):
            w2(hf, dr, item, False).wait_send()
    every(lambda d: row_copy(st_out, st_in, st_s, st_r, d, False).wait_send())
    every(lambda d: column_copy(d, False).wait_send())
    every(lambda d: row_copy(ret_out, ret_in, ret_s, ret_r, d, False).wait_send())
    for o in range(4):
        sib_copy(o).wait_send()
    for way in (0, 1):
        x1_copy(way).wait_send()
        for part in (0, 1):
            x2_copy(way, part).wait_send()


def per_device(
    x_in, gate_z, b_in, c_in, step_size, log_decay, d_skip, norm_gain, query, key, value, o_weight
):
    vmem = pl.BlockSpec(memory_space=pltpu.VMEM)
    smem = pl.BlockSpec(memory_space=pltpu.SMEM)
    hbm = pl.BlockSpec(memory_space=pl.ANY)
    dma = pltpu.SemaphoreType.DMA
    tokens = (TOK, 512)
    return pl.pallas_call(
        kernel,
        out_shape=(jax.ShapeDtypeStruct(tokens, BF), jax.ShapeDtypeStruct(tokens, BF)),
        in_specs=[hbm] * 6 + [smem, vmem] + [hbm] * 4,
        out_specs=(vmem, vmem),
        scratch_shapes=[
            pltpu.VMEM(tokens, BF),
            pltpu.VMEM(tokens, BF),
            pltpu.VMEM((TOK, ADH), BF),
            pltpu.VMEM((TOK, ADH), BF),
            pltpu.VMEM((8, TOK), F32),
            pltpu.VMEM((8, TOK), F32),
            pltpu.VMEM((2, RING, 2, TOK, ADH), BF),
            pltpu.VMEM((2, RING, 2, TOK, ADH), BF),
            pltpu.VMEM((2, RING, RING, 64, 256), BF),
            pltpu.VMEM((2, 2, TOK, 2 * ADH), F32),
            pltpu.VMEM((2, 2, TOK, ADH), F32),
            pltpu.VMEM((2, RING, 2, TOK, ADH), F32),
            pltpu.VMEM((2, RING, 2, TOK, ADH), F32),
            pltpu.VMEM((2, 2, 4, 2, TOK, ADH), BF),
            pltpu.VMEM((2, 2, 4, 8, ADH), F32),
            pltpu.VMEM((2, 2, 4, 2, TOK, ADH), BF),
            pltpu.VMEM((2, 2, 4, 8, ADH), F32),
            pltpu.VMEM(tokens, BF),
            pltpu.VMEM((8, TOK), F32),
            pltpu.VMEM((TOK, TOK), F32),
            pltpu.VMEM(tokens, F32),
            pltpu.VMEM((TOK, ADH), F32),
            pltpu.VMEM((RING, 80, ADH), BF),
            pltpu.VMEM((RING, 80, ADH), BF),
            pltpu.VMEM((RING, 64, ADH), F32),
            pltpu.VMEM((RING, 8, ADH), F32),
            pltpu.VMEM((80, ADH), BF),
            pltpu.VMEM((RING, 80, ADH), BF),
            pltpu.VMEM((RING, 64, ADH), BF),
            pltpu.VMEM((RING, 64, ADH), BF),
            pltpu.VMEM((XS,) + tokens, BF),
            pltpu.VMEM((XS,) + tokens, BF),
            pltpu.VMEM((XS,) + tokens, BF),
            pltpu.VMEM((2, HALF, 512), BF),
            pltpu.VMEM((2, HALF, 512), BF),
            pltpu.VMEM((2,) + tokens, BF),
            pltpu.VMEM((2,) + tokens, BF),
            dma((11,)), dma((8,)), dma((8,)), dma((2,)), dma((2,)), dma, dma, dma((2, 4)), dma((2, 4)),
            dma((2, 2, 4)), dma((2, 2, 4)), dma((2, 2, 4)), dma((2, 2, 4)), dma((2, 2, 4)), dma((2, 2, 4)),
            dma((2, 8)), dma((2, 8)), dma((2, 2, 7)), dma((2, 2, 7)),
            dma((8,)), dma((8,)), dma((8,)), dma((8,)), dma((8,)), dma((8,)),
            dma((4,)), dma((4,)), dma((2,)), dma((2,)), dma((2, 2)), dma((2, 2)),
        ],
        compiler_params=pltpu.CompilerParams(
            collective_id=0, has_side_effects=True, vmem_limit_bytes=60 * 1024 * 1024
        ),
        name="mixer_and_attention",
    )(
        x_in, gate_z, b_in, c_in, step_size, log_decay, d_skip, norm_gain.reshape(1, 512),
        query, key, value, o_weight.T,
    )


def solution(mesh):
    in_specs = (
        P("ctx", "head"),
        P("ctx", "head"),
        P("ctx", "head"),
        P("ctx", "head"),
        P("head", "ctx"),
        P("head", "ctx"),
        P("head"),
        P("head"),
        P("ctx", "head"),
        P("ctx", "head"),
        P("ctx", "head"),
        P("head", "ctx"),
    )
    out_specs = (P("ctx", "head"), P("ctx", "head"))
    return jax.shard_map(
        per_device, mesh=mesh, in_specs=in_specs, out_specs=out_specs, check_vma=False
    )
```

```python
import functools
import math

import jax
import jax.numpy as jnp
from jax import lax
from jax.experimental import pallas as pl
from jax.experimental.pallas import tpu as pltpu
from jax.sharding import PartitionSpec as P

MESH = pl.DeviceIdType.MESH
BF = jnp.bfloat16
F32 = jnp.float32
TOK = 256
HALF = TOK // 2
ADH = 128
SHARE = 4
RING = 8
XS = 4
NEG = -1e30
SCALE = math.log2(math.e) / math.sqrt(ADH)
NT = (((1,), (1,)), ((), ()))


def mod(a, n):
    return lax.rem(a + 2 * n, n)


def dot(a, b):
    return jnp.dot(a, b, preferred_element_type=F32)


def dot_nt(a, b, precision=None):
    return lax.dot_general(a, b, NT, precision=precision, preferred_element_type=F32)


def kernel(
    x_hbm, gate_hbm, b_hbm, c_hbm, step_hbm, decay_hbm, skip_ref, gain_ref, q_hbm, k_hbm, v_hbm, wt_hbm,
    ssm_ref, out_ref,
    x_ref, gate_ref, b_ref, c_ref, step_ref, decay_ref,
    kv, qs, w, acc, peak, part_o, part_l, tx_o, tx_l, rx_o, rx_l, heads,
    arow, scores, gated, squares, st_out, st_in, pre, predec, tot_out, tot_in, ret_out, ret_in,
    sib_out, sib_in, mine, x1_out, x1_in, x2_out, x2_in,
    in_s, skv_s, skv_r, sq_s, sq_r, sw_s, sw_r, kr_s, kr_r, qr_s, qr_r, o_s, o_r, l_s, l_r,
    w1_s, w1_r, w2_s, w2_r,
    st_s, st_r, tot_s, tot_r, ret_s, ret_r, sib_s, sib_r, x1_s, x1_r, x2_s, x2_r,
):
    me = lax.axis_index("ctx")
    head = lax.axis_index("head")
    y, z = me // RING, me % RING
    xc, core = head // 2, head % 2
    sibling = (me, 2 * xc + 1 - core)
    major0, minor0 = (y, z), (z, y)

    def q_place(m):
        return jnp.where(m == 0, z, y)

    def k_place(m):
        return jnp.where(m == 0, y, z)

    def ctx_at(m, q, k):
        return jnp.where(m == 0, k * RING + q, q * RING + k)

    def ctx_of(hf, major, minor):
        return major * RING + minor if hf == 0 else minor * RING + major

    barrier = pltpu.get_barrier_semaphore()

    def greet(i, _):
        pl.semaphore_signal(barrier, inc=1, device_id=(y * RING + mod(z + i, RING), head), device_id_type=MESH)
        pl.semaphore_signal(barrier, inc=1, device_id=(mod(y + i, RING) * RING + z, head), device_id_type=MESH)
        pl.semaphore_signal(barrier, inc=1, device_id=(me, mod(head + i, 8)), device_id_type=MESH)
        return 0

    lax.fori_loop(1, 8, greet, 0)

    my_k, my_q = k_place(core), q_place(core)

    def lanes(block, width):
        return pl.ds(pl.multiple_of(block * width, width), width)

    fetches = [
        (k_hbm, kv.at[core, my_k, 0]),
        (v_hbm, kv.at[core, my_k, 1]),
        (q_hbm.at[:, lanes(2 * core, ADH)], qs.at[core, my_q, 0]),
        (q_hbm.at[:, lanes(2 * core + 1, ADH)], qs.at[core, my_q, 1]),
        (wt_hbm.at[:, lanes(core, 256)], w.at[core, my_k, my_q]),
        (decay_hbm, decay_ref),
        (b_hbm, b_ref),
        (x_hbm, x_ref),
        (step_hbm, step_ref),
        (c_hbm, c_ref),
        (gate_hbm, gate_ref),
    ]
    fetches = [pltpu.make_async_copy(src, dst, in_s.at[i]) for i, (src, dst) in enumerate(fetches)]
    for fetch in fetches:
        fetch.start()
    for fetch in fetches[:2]:
        fetch.wait()
    pl.semaphore_wait(barrier, 21)

    def sib_kv(m, place):
        ref = kv.at[m, place]
        return pltpu.make_async_remote_copy(
            src_ref=ref, dst_ref=ref, send_sem=skv_s.at[place], recv_sem=skv_r.at[place],
            device_id=sibling, device_id_type=MESH,
        )

    def sib_q(m, i):
        return pltpu.make_async_remote_copy(
            src_ref=q_hbm.at[:, lanes(2 * (1 - core) + i, ADH)], dst_ref=qs.at[m, q_place(m), i],
            send_sem=sq_s.at[i], recv_sem=sq_r.at[i], device_id=sibling, device_id_type=MESH,
        )

    def sib_w(m):
        return pltpu.make_async_remote_copy(
            src_ref=wt_hbm.at[:, lanes(1 - core, 256)], dst_ref=w.at[m, k_place(m), q_place(m)],
            send_sem=sw_s, recv_sem=sw_r, device_id=sibling, device_id_type=MESH,
        )

    def ring_kv(dr, dist, part, arriving):
        way = 0 if dr > 0 else 1
        place = mod(my_k - dr * (dist if arriving else dist - 1), RING)
        ref = kv.at[core, place, part]
        to = ctx_at(core, my_q, mod(my_k + dr, RING))
        at = (way, dist - 1, part)
        return pltpu.make_async_remote_copy(
            src_ref=ref, dst_ref=ref, send_sem=kr_s.at[at], recv_sem=kr_r.at[at],
            device_id=(to, head), device_id_type=MESH,
        )

    def ring_q(m, dr, dist, part, arriving):
        way = 0 if dr > 0 else 1
        place = mod(q_place(m) - dr * (dist if arriving else dist - 1), RING)
        ref = qs.at[m, place, part]
        to = ctx_at(m, mod(q_place(m) + dr, RING), k_place(m))
        at = (m, way, dist - 1, part)
        return pltpu.make_async_remote_copy(
            src_ref=ref, dst_ref=ref, send_sem=qr_s.at[at], recv_sem=qr_r.at[at],
            device_id=(to, head), device_id_type=MESH,
        )

    def goes(dr, dist, part):
        return dist < 4 or (dist == 4 and part == (0 if dr > 0 else 1))

    def kv_hop(dist):
        for part in (0, 1):
            for dr in (1, -1):
                if dist > 0 and goes(dr, dist, part):
                    ring_kv(dr, dist, part, True).wait_recv()
                if goes(dr, dist + 1, part):
                    ring_kv(dr, dist + 1, part, False).start()
        if dist > 0:
            for dr in (1, -1) if dist < 4 else (1,):
                sib_kv(core, mod(my_k - dr * dist, RING)).start()

    def q_hop(dist, part):
        for m in (0, 1):
            for dr in (1, -1):
                if dist > 0 and goes(dr, dist, part):
                    ring_q(m, dr, dist, part, True).wait_recv()
                if goes(dr, dist + 1, part):
                    ring_q(m, dr, dist + 1, part, False).start()

    def first(buf, ss, rs, hf, dr, dist, arriving):
        slot = dist - 1 + (0 if dr > 0 else 4)
        block = mod(minor0[hf] - dr * (dist if arriving else dist - 1), RING)
        ref = buf.at[hf, major0[hf], block]
        to = ctx_of(hf, major0[hf], mod(minor0[hf] + dr, RING))
        return pltpu.make_async_remote_copy(
            src_ref=ref, dst_ref=ref, send_sem=ss.at[hf, slot], recv_sem=rs.at[hf, slot],
            device_id=(to, head), device_id_type=MESH,
        )

    def second(buf, ss, rs, hf, dr, dist, pair, arriving):
        way = 0 if dr > 0 else 1
        major = mod(major0[hf] - dr * (dist if arriving else dist - 1), RING)
        two = mod(minor0[hf] // 2 + (0, 1, 3, 2)[pair], RING // 2)
        ref = buf.at[hf, major, pl.ds(2 * two, 2)]
        to = ctx_of(hf, mod(major0[hf] + dr, RING), minor0[hf])
        at = (hf, way, dist - 1, pair)
        return pltpu.make_async_remote_copy(
            src_ref=ref, dst_ref=ref, send_sem=ss.at[at], recv_sem=rs.at[at],
            device_id=(to, head), device_id_type=MESH,
        )

    STREAMS = [(hf, dr) for hf in (0, 1) for dr in (1, -1)]
    reach = {(0, 1): 4, (0, -1): 3, (1, 1): 3, (1, -1): 4}
    w1 = functools.partial(first, w, w1_s, w1_r)
    w2 = functools.partial(second, w, w2_s, w2_r)

    def w_hop(dist):
        for hf, dr in STREAMS:
            if 0 < dist <= reach[hf, dr]:
                w1(hf, dr, dist, True).wait_recv()
            if dist < reach[hf, dr]:
                w1(hf, dr, dist + 1, False).start()

    def w_goes(dr, dist, pair):
        return dist < 4 or (dist == 4 and (pair < 2) == (dr > 0))

    def w_pass(dist, pair):
        for hf, dr in STREAMS:
            if dist > 0 and w_goes(dr, dist, pair):
                w2(hf, dr, dist, pair, True).wait_recv()
            if w_goes(dr, dist + 1, pair):
                w2(hf, dr, dist + 1, pair, False).start()

    kv_hop(0)
    sib_kv(core, my_k).start()
    for i in (0, 1):
        sib_q(core, i).start()
    sib_w(core).start()
    for fetch in fetches[2:5]:
        fetch.wait()

    def weigh(m, i, s, v, fresh):
        n = s.shape[1]
        top = jnp.broadcast_to(jnp.max(s, axis=1, keepdims=True) * SCALE, (TOK, ADH))
        new = top if fresh else jnp.maximum(peak[m, i], top)
        p = jnp.exp2(s * SCALE - jnp.concatenate([new] * (n // ADH), axis=1)).astype(BF)
        pv = dot(p, jnp.concatenate([v, jnp.ones((n, ADH), BF)], axis=1))
        if fresh:
            acc[m, i] = pv
        else:
            shrink = jnp.exp2(peak[m, i] - new)
            acc[m, i] = acc[m, i] * jnp.concatenate([shrink, shrink], axis=1) + pv
        peak[m, i] = new

    rows = lax.broadcasted_iota(jnp.int32, (TOK, TOK), 0)
    cols = lax.broadcasted_iota(jnp.int32, (TOK, TOK), 1)
    causal = rows >= cols

    def own_block(m, _):
        at, q = k_place(m), q_place(m)
        for i in (0, 1):
            s = jnp.where(causal, dot_nt(qs[m, q, i], kv[m, at, 0]), NEG)
            weigh(2 + m, i, s, kv[m, at, 1], True)
        return 0

    def tile(step):
        near_by = 4 - (step + 1) // 2
        away = jnp.where(step % 2 == 1, near_by, mod(RING - near_by, RING))

        def one(m, _):
            q = mod(q_place(m) + away, RING)
            at_z = y + jnp.where(q > z, 1, 0)
            at_y = jnp.where(q > y, RING, jnp.where(q == y, z, 0))
            blocks = jnp.where(m == 0, at_z, at_y)

            t_at = jnp.where(step == 7, 2 + m, m)

            @pl.when(step < 7)
            def _():
                acc[m] = jnp.zeros((2, TOK, 2 * ADH), F32)
                peak[m] = jnp.full((2, TOK, ADH), NEG, F32)

            def keys(t, _):
                ks = kv[m, pl.ds(2 * t, 2), 0].reshape(2 * TOK, ADH)
                vs = kv[m, pl.ds(2 * t, 2), 1].reshape(2 * TOK, ADH)
                both = [dot_nt(qs[m, q, i], ks) for i in (0, 1)]
                for i in (0, 1):
                    weigh(t_at, i, both[i], vs, False)
                return 0

            lax.fori_loop(0, blocks // 2, keys, 0)

            @pl.when(blocks % 2 == 1)
            def _():
                ks, vs = kv[m, blocks - 1, 0], kv[m, blocks - 1, 1]
                both = [dot_nt(qs[m, q, i], ks) for i in (0, 1)]
                for i in (0, 1):
                    weigh(t_at, i, both[i], vs, False)

            for i in (0, 1):
                total = jnp.maximum(acc[t_at, i][:, ADH:], 1e-30)
                part_o[m, away, i] = acc[t_at, i][:, :ADH] / total
                part_l[m, away, i] = peak[t_at, i] + jnp.log2(total)
            return 0

        lax.fori_loop(0, 2, one, 0)

    small = lax.broadcasted_iota(jnp.int32, (ADH, ADH), 0) == lax.broadcasted_iota(jnp.int32, (ADH, ADH), 1)

    def packed(l):
        halves = [l[r * ADH : (r + 1) * ADH] for r in (0, 1)]
        return [jnp.sum(jnp.where(small, half, 0.0), axis=0, keepdims=True) for half in halves]

    def unpacked(block):
        halves = []
        for r in (0, 1):
            row = jnp.broadcast_to(block[r : r + 1], (ADH, ADH))
            column = jnp.sum(jnp.where(small, row, 0.0), axis=1, keepdims=True)
            halves.append(jnp.broadcast_to(column, (ADH, ADH)))
        return jnp.concatenate(halves, axis=0)

    def join(o1, l1, o2, l2):
        top = jnp.maximum(l1, l2)
        w1_, w2_ = jnp.exp2(l1 - top), jnp.exp2(l2 - top)
        total = w1_ + w2_
        return (o1 * w1_ + o2 * w2_) / total, top + jnp.log2(total)

    def back_copies(m, way, k, i):
        at = (m, way, k - 1, i)
        to = ctx_at(m, mod(q_place(m) + (1 if way == 0 else -1), RING), k_place(m))
        return [
            pltpu.make_async_remote_copy(
                src_ref=out.at[at], dst_ref=into.at[at], send_sem=ss.at[at], recv_sem=rs.at[at],
                device_id=(to, head), device_id_type=MESH,
            )
            for out, into, ss, rs in ((tx_o, rx_o, o_s, o_r), (tx_l, rx_l, l_s, l_r))
        ]

    def came(m, way, k, i):
        for copy in back_copies(m, way, k, i):
            copy.wait_recv()
        return rx_o[m, way, k - 1, i].astype(F32), unpacked(rx_l[m, way, k - 1, i])

    def back(k, way, i):
        away = k if way == 0 else RING - k

        def one(m, _):
            o, l = part_o[m, away, i], part_l[m, away, i]
            if k < 3 or (k == 3 and i == way):
                o, l = join(o, l, *came(m, way, k + 1, i))
            tx_o[m, way, k - 1, i] = o.astype(BF)
            tx_l[m, way, k - 1, i] = jnp.concatenate(packed(l) + [jnp.zeros((6, ADH), F32)], axis=0)
            for copy in back_copies(m, way, k, i):
                copy.start()
            return 0

        lax.fori_loop(0, 2, one, 0)

    def collect():
        for i in (0, 1):
            for m in (0, 1):
                o, l = part_o[m, 0, i], part_l[m, 0, i]
                for way in (0, 1):
                    o, l = join(o, l, *came(m, way, 1, i))
                f = 2 * m + i
                heads[:, f * ADH : (f + 1) * ADH] = o.astype(BF)

    lane = lax.broadcasted_iota(jnp.int32, (1, ADH), 1) < 64

    def tri():
        return jnp.where(causal, 1.0, 0.0).astype(F32)

    def spread(pair):
        rows2 = [jnp.broadcast_to(decay_ref[pl.ds(2 * pair + i, 1), :], (64, TOK)) for i in (0, 1)]
        return dot_nt(tri(), jnp.concatenate(rows2, axis=0), lax.Precision.HIGHEST)

    def pair_columns(pair):
        return lanes(pair, ADH)

    def split(vec):
        hi = vec.astype(BF)
        lo = (vec - hi.astype(F32)).astype(BF)
        return jnp.concatenate([jnp.broadcast_to(hi, (8, ADH)), jnp.broadcast_to(lo, (8, ADH))], axis=0)

    def joined(block):
        return block[64:65].astype(F32) + block[72:73].astype(F32)

    def row_copy(out, into, ss, rs, dz, arriving):
        there = mod(z + dz, RING)
        src = mod(z - dz, RING) if arriving else z
        return pltpu.make_async_remote_copy(
            src_ref=out.at[there], dst_ref=into.at[src], send_sem=ss.at[dz], recv_sem=rs.at[dz],
            device_id=(y * RING + there, head), device_id_type=MESH,
        )

    def column_copy(dy, arriving):
        there = mod(y + dy, RING)
        src = mod(y - dy, RING) if arriving else y
        return pltpu.make_async_remote_copy(
            src_ref=tot_out, dst_ref=tot_in.at[src], send_sem=tot_s.at[dy], recv_sem=tot_r.at[dy],
            device_id=(there * RING + z, head), device_id_type=MESH,
        )

    def every(f):
        def one(i, _):
            f(i)
            return 0

        lax.fori_loop(1, RING, one, 0)

    def states_out():
        arow[...] = dot_nt(decay_ref[...], tri(), lax.Precision.HIGHEST)
        bt = b_ref[...].astype(F32).T

        def one(pair, _):
            xp = x_ref[:, pair_columns(pair)]
            parts = []
            for i in (0, 1):
                a = arow[pl.ds(2 * pair + i, 1), :]
                tail = jnp.exp(a - a[:, TOK - 1 :]) * step_ref[pl.ds(2 * pair + i, 1), :]
                parts.append(dot((bt * tail).astype(BF), xp))
            state = jnp.where(lane, parts[0], parts[1]).astype(BF)
            last = [arow[pl.ds(2 * pair + i, 1), :][:, TOK - 1 :] for i in (0, 1)]
            through = split(jnp.exp(-jnp.where(lane, last[0], last[1])))
            for i in (0, 1):
                st_out[2 * pair + i, :64] = state[64 * i : 64 * i + 64]
                st_out[2 * pair + i, 64:] = through
            return 0

        lax.fori_loop(0, 4, one, 0)
        st_in[z] = st_out[z]

    def totals_out():
        every(lambda dz: row_copy(st_out, st_in, st_s, st_r, dz, True).wait_recv())

        def one(i, carry):
            state, decay = carry
            pre[i] = state
            predec[i] = jnp.broadcast_to(decay, (8, ADH))
            block = st_in[i]
            t = joined(block)
            return t * state + block[:64].astype(F32), t * decay

        state, decay = lax.fori_loop(0, RING, one, (jnp.zeros((64, ADH), F32), jnp.ones((1, ADH), F32)))
        tot_out[:64] = state.astype(BF)
        tot_out[64:] = split(decay)
        every(lambda dy: column_copy(dy, False).start())

    def incoming_out():
        every(lambda dy: column_copy(dy, True).wait_recv())

        def one(i, state):
            block = tot_in[i]
            return joined(block) * state + block[:64].astype(F32)

        state = lax.fori_loop(0, y, one, jnp.zeros((64, ADH), F32))

        def give(i, _):
            ret_out[i] = (pre[i] + predec[i][:1] * state).astype(BF)
            return 0

        lax.fori_loop(0, RING, give, 0)
        every(lambda dz: row_copy(ret_out, ret_in, ret_s, ret_r, dz, False).start())
        ret_in[z] = ret_out[z]

    def mix_pair(pair):
        if pair == 0:
            every(lambda dz: row_copy(ret_out, ret_in, ret_s, ret_r, dz, True).wait_recv())
            scores[...] = dot_nt(c_ref[...], b_ref[...])
            squares[...] = jnp.zeros_like(squares)

        at = pair_columns(pair)
        xp = x_ref[:, at]
        a_t = spread(pair)
        parts = []
        for i in (0, 1):
            a_u = arow[pl.ds(2 * pair + i, 1), :]
            gap = jnp.where(causal, a_u - a_t[:, 64 * i : 64 * i + 1], NEG)
            mixing = jnp.exp(gap) * (scores[...] * step_ref[pl.ds(2 * pair + i, 1), :])
            parts.append(dot(mixing.astype(BF), xp))
        carried = dot(c_ref[...], ret_in[pl.ds(2 * pair, 2)].reshape(ADH, ADH)) * jnp.exp(-a_t)
        skip = jnp.where(lane, skip_ref[2 * pair], skip_ref[2 * pair + 1])
        total = jnp.where(lane, parts[0], parts[1]) + carried + skip * xp.astype(F32)
        g = gate_ref[:, at].astype(F32)
        total = total * (g / (1.0 + jnp.exp(-g)))
        gated[:, at] = total
        squares[...] += jnp.broadcast_to(jnp.sum(total * total, axis=1, keepdims=True), (TOK, ADH))

    def mix_end():
        norm = lax.rsqrt(squares[...] / 512.0 + 1e-05)
        norm = jnp.concatenate([norm] * 4, axis=1)
        ssm_ref[...] = (gated[...] * norm * gain_ref[...].astype(F32)).astype(BF)

    for i in (0, 1):
        sib_q(1 - core, i).wait_recv()
        if i == 1:
            for fetch in fetches[5:]:
                fetch.wait()
            states_out()
        q_hop(0, i)
    sib_w(1 - core).wait_recv()
    w_hop(0)
    kv_hop(1)
    q_hop(1, 0)
    every(lambda dz: row_copy(st_out, st_in, st_s, st_r, dz, False).start())
    sib_kv(1 - core, k_place(1 - core)).wait_recv()
    lax.fori_loop(0, 2, own_block, 0)
    q_hop(1, 1)
    w_hop(1)
    w_pass(0, 0)
    for dist in (2, 3, 4):
        kv_hop(dist)
        q_hop(dist, 0)
        q_hop(dist, 1)
        w_hop(dist)
        if dist == 3:
            w_pass(0, 1)
            w_pass(0, 2)
            w_pass(1, 0)
            totals_out()
    w_pass(0, 3)
    w_pass(2, 0)

    def rest(i, _):
        sib_kv(1 - core, mod(k_place(1 - core) + i, RING)).wait_recv()
        return 0

    lax.fori_loop(1, RING, rest, 0)

    TURNS = (
        (), ((1, 1),), ((1, 2), (1, 3)), ((3, 0), (2, 1)),
        ((2, 2), (2, 3)), ((4, 0), (3, 1)), ((3, 2), (3, 3)), ((4, 1), (4, 2)),
    )

    def step(i, _):
        for at, turns in enumerate(TURNS):

            @pl.when(i == at)
            def _(turns=turns):
                for turn in turns:
                    w_pass(*turn)

        pl.when(i == 1)(incoming_out)
        tile(i)

        @pl.when(i == 0)
        def _():
            back(4, 0, 0)
            back(4, 1, 1)

        for k in (3, 2, 1):
            for way in (0, 1):

                @pl.when(i == 7 - 2 * k + way)
                def _(k=k, way=way):
                    back(k, way, 1 - way)
                    back(k, way, way)

        return 0

    lax.fori_loop(0, 8, step, 0)
    collect()
    w_pass(4, 3)

    def product(f):
        left = dot_nt(heads[:, :256], w[0, f].reshape(512, 256))
        right = dot_nt(heads[:, 256:], w[1, :, f].reshape(512, 256))
        return (left + right).astype(BF)

    def sib_copy(o):
        return pltpu.make_async_remote_copy(
            src_ref=sib_out.at[o], dst_ref=sib_in.at[o], send_sem=sib_s.at[o], recv_sem=sib_r.at[o],
            device_id=(me, 2 * xc + 1 - core), device_id_type=MESH,
        )

    def side(way):
        return (me, 2 * mod(xc + (1 if way == 0 else -1), XS) + core)

    def x1_copy(way):
        return pltpu.make_async_remote_copy(
            src_ref=x1_out.at[way], dst_ref=x1_in.at[way], send_sem=x1_s.at[way], recv_sem=x1_r.at[way],
            device_id=side(way), device_id_type=MESH,
        )

    def x2_copy(way, part):
        ref = (way, pl.ds(part * HALF, HALF))
        return pltpu.make_async_remote_copy(
            src_ref=x2_out.at[ref], dst_ref=x2_in.at[ref], send_sem=x2_s.at[way, part], recv_sem=x2_r.at[way, part],
            device_id=side(way), device_id_type=MESH,
        )

    def for_sibling(o):
        sib_out[o] = product(2 * mod(xc + o, XS) + 1 - core)
        sib_copy(o).start()

    def for_own(o):
        mine[o] = product(2 * mod(xc + o, XS) + core)

    def both(o, part):
        at = pl.ds(part * HALF, HALF)
        return mine[o, at].astype(F32) + sib_in[o, at].astype(F32)

    for_sibling(2)
    for_own(2)
    for_sibling(1)
    for_sibling(3)
    sib_copy(2).wait_recv()
    for way in (0, 1):
        x1_out[way] = both(2, way).astype(BF)
        x1_copy(way).start()
    for way, o in ((0, 1), (1, 3)):
        for_own(o)
        sib_copy(o).wait_recv()
        x2_out[way, (1 - way) * HALF : (2 - way) * HALF] = both(o, 1 - way).astype(BF)
        x2_copy(way, 1 - way).start()
    mix_pair(0)
    mix_pair(1)
    for way, o in ((0, 1), (1, 3)):
        x1_copy(way).wait_recv()
        x2_out[way, way * HALF : (way + 1) * HALF] = (both(o, way) + x1_in[way].astype(F32)).astype(BF)
        x2_copy(way, way).start()
    for_sibling(0)
    for_own(0)
    mix_pair(2)
    mix_pair(3)
    mix_end()
    sib_copy(0).wait_recv()
    for part in (1, 0):
        x2_copy(0, part).wait_recv()
        x2_copy(1, part).wait_recv()
    for part in (0, 1):
        at = pl.ds(part * HALF, HALF)
        out_ref[at] = (both(0, part) + x2_in[0, at].astype(F32) + x2_in[1, at].astype(F32)).astype(BF)

    def sent(i, _):
        sib_kv(core, i).wait_send()
        return 0

    lax.fori_loop(0, RING, sent, 0)
    for i in (0, 1):
        sib_q(core, i).wait_send()
    sib_w(core).wait_send()
    for k in range(1, 5):
        for way, dr in ((0, 1), (1, -1)):
            for part in (0, 1):
                if goes(dr, k, part):
                    ring_kv(dr, k, part, False).wait_send()

    def sent_both(m, _):
        for k in range(1, 5):
            for way, dr in ((0, 1), (1, -1)):
                for part in (0, 1):
                    if goes(dr, k, part):
                        ring_q(m, dr, k, part, False).wait_send()
                        for copy in back_copies(m, way, k, part):
                            copy.wait_send()
        return 0

    lax.fori_loop(0, 2, sent_both, 0)
    for hf, dr in STREAMS:
        for dist in range(1, reach[hf, dr] + 1):
            w1(hf, dr, dist, False).wait_send()
        for dist in range(1, 5):
            for pair in range(4):
                if w_goes(dr, dist, pair):
                    w2(hf, dr, dist, pair, False).wait_send()
    every(lambda d: row_copy(st_out, st_in, st_s, st_r, d, False).wait_send())
    every(lambda d: column_copy(d, False).wait_send())
    every(lambda d: row_copy(ret_out, ret_in, ret_s, ret_r, d, False).wait_send())
    for o in range(4):
        sib_copy(o).wait_send()
    for way in (0, 1):
        x1_copy(way).wait_send()
        for part in (0, 1):
            x2_copy(way, part).wait_send()


def per_device(
    x_in, gate_z, b_in, c_in, step_size, log_decay, d_skip, norm_gain, query, key, value, o_weight
):
    vmem = pl.BlockSpec(memory_space=pltpu.VMEM)
    smem = pl.BlockSpec(memory_space=pltpu.SMEM)
    hbm = pl.BlockSpec(memory_space=pl.ANY)
    dma = pltpu.SemaphoreType.DMA
    tokens = (TOK, 512)
    return pl.pallas_call(
        kernel,
        out_shape=(jax.ShapeDtypeStruct(tokens, BF), jax.ShapeDtypeStruct(tokens, BF)),
        in_specs=[hbm] * 6 + [smem, vmem] + [hbm] * 4,
        out_specs=(vmem, vmem),
        scratch_shapes=[
            pltpu.VMEM(tokens, BF),
            pltpu.VMEM(tokens, BF),
            pltpu.VMEM((TOK, ADH), BF),
            pltpu.VMEM((TOK, ADH), BF),
            pltpu.VMEM((8, TOK), F32),
            pltpu.VMEM((8, TOK), F32),
            pltpu.VMEM((2, RING, 2, TOK, ADH), BF),
            pltpu.VMEM((2, RING, 2, TOK, ADH), BF),
            pltpu.VMEM((2, RING, RING, 64, 256), BF),
            pltpu.VMEM((4, 2, TOK, 2 * ADH), F32),
            pltpu.VMEM((4, 2, TOK, ADH), F32),
            pltpu.VMEM((2, RING, 2, TOK, ADH), F32),
            pltpu.VMEM((2, RING, 2, TOK, ADH), F32),
            pltpu.VMEM((2, 2, 4, 2, TOK, ADH), BF),
            pltpu.VMEM((2, 2, 4, 2, 8, ADH), F32),
            pltpu.VMEM((2, 2, 4, 2, TOK, ADH), BF),
            pltpu.VMEM((2, 2, 4, 2, 8, ADH), F32),
            pltpu.VMEM(tokens, BF),
            pltpu.VMEM((8, TOK), F32),
            pltpu.VMEM((TOK, TOK), F32),
            pltpu.VMEM(tokens, F32),
            pltpu.VMEM((TOK, ADH), F32),
            pltpu.VMEM((RING, 80, ADH), BF),
            pltpu.VMEM((RING, 80, ADH), BF),
            pltpu.VMEM((RING, 64, ADH), F32),
            pltpu.VMEM((RING, 8, ADH), F32),
            pltpu.VMEM((80, ADH), BF),
            pltpu.VMEM((RING, 80, ADH), BF),
            pltpu.VMEM((RING, 64, ADH), BF),
            pltpu.VMEM((RING, 64, ADH), BF),
            pltpu.VMEM((XS,) + tokens, BF),
            pltpu.VMEM((XS,) + tokens, BF),
            pltpu.VMEM((XS,) + tokens, BF),
            pltpu.VMEM((2, HALF, 512), BF),
            pltpu.VMEM((2, HALF, 512), BF),
            pltpu.VMEM((2,) + tokens, BF),
            pltpu.VMEM((2,) + tokens, BF),
            dma((11,)), dma((8,)), dma((8,)), dma((2,)), dma((2,)), dma, dma, dma((2, 4, 2)), dma((2, 4, 2)),
            *[dma((2, 2, 4, 2))] * 6,
            dma((2, 8)), dma((2, 8)), dma((2, 2, 4, 4)), dma((2, 2, 4, 4)),
            dma((8,)), dma((8,)), dma((8,)), dma((8,)), dma((8,)), dma((8,)),
            dma((4,)), dma((4,)), dma((2,)), dma((2,)), dma((2, 2)), dma((2, 2)),
        ],
        compiler_params=pltpu.CompilerParams(
            collective_id=0, has_side_effects=True, vmem_limit_bytes=60 * 1024 * 1024
        ),
        name="mixer_and_attention",
    )(
        x_in, gate_z, b_in, c_in, step_size, log_decay, d_skip, norm_gain.reshape(1, 512),
        query, key, value, o_weight.T,
    )


def solution(mesh):
    in_specs = (
        P("ctx", "head"),
        P("ctx", "head"),
        P("ctx", "head"),
        P("ctx", "head"),
        P("head", "ctx"),
        P("head", "ctx"),
        P("head"),
        P("head"),
        P("ctx", "head"),
        P("ctx", "head"),
        P("ctx", "head"),
        P("head", "ctx"),
    )
    out_specs = (P("ctx", "head"), P("ctx", "head"))
    return jax.shard_map(
        per_device, mesh=mesh, in_specs=in_specs, out_specs=out_specs, check_vma=False
    )
```

```python
import functools
import math

import jax
import jax.numpy as jnp
from jax import lax
from jax.experimental import pallas as pl
from jax.experimental.pallas import tpu as pltpu
from jax.sharding import PartitionSpec as P

MESH = pl.DeviceIdType.MESH
BF = jnp.bfloat16
F32 = jnp.float32
TOK = 256
HALF = TOK // 2
ADH = 128
SHARE = 4
RING = 8
XS = 4
NEG = -1e30
SCALE = math.log2(math.e) / math.sqrt(ADH)
NT = (((1,), (1,)), ((), ()))


def mod(a, n):
    return lax.rem(a + 2 * n, n)


def dot(a, b):
    return jnp.dot(a, b, preferred_element_type=F32)


def dot_nt(a, b, precision=None):
    return lax.dot_general(a, b, NT, precision=precision, preferred_element_type=F32)


def kernel(
    x_hbm, gate_hbm, b_hbm, c_hbm, step_hbm, decay_hbm, skip_hbm, gain_ref, q_hbm, k_hbm, v_hbm, wt_hbm,
    ssm_ref, out_ref,
    x_ref, gate_ref, b_ref, c_ref, step_ref, decay_ref, skip_ref,
    kv, qs, w, acc, peak, part_o, part_l, tx_o, tx_l, rx_o, rx_l, heads,
    arow, scores, gated, squares, st_out, st_in, pre, predec, tot_out, tot_in, ret_out, ret_in,
    sib_out, sib_in, mine, x1_out, x1_in, x2_out, x2_in,
    in_s, skv_s, skv_r, sq_s, sq_r, sw_s, sw_r, kr_s, kr_r, qr_s, qr_r, o_s, o_r, l_s, l_r,
    w1_s, w1_r, w2_s, w2_r,
    st_s, st_r, tot_s, tot_r, ret_s, ret_r, sib_s, sib_r, x1_s, x1_r, x2_s, x2_r,
):
    me = lax.axis_index("ctx")
    head = lax.axis_index("head")
    y, z = me // RING, me % RING
    xc, core = head // 2, head % 2
    sibling = (me, 2 * xc + 1 - core)
    major0, minor0 = (y, z), (z, y)

    def q_place(m):
        return jnp.where(m == 0, z, y)

    def k_place(m):
        return jnp.where(m == 0, y, z)

    def ctx_at(m, q, k):
        return jnp.where(m == 0, k * RING + q, q * RING + k)

    def ctx_of(hf, major, minor):
        return major * RING + minor if hf == 0 else minor * RING + major

    barrier = pltpu.get_barrier_semaphore()

    def greet(i, _):
        pl.semaphore_signal(barrier, inc=1, device_id=(y * RING + mod(z + i, RING), head), device_id_type=MESH)
        pl.semaphore_signal(barrier, inc=1, device_id=(mod(y + i, RING) * RING + z, head), device_id_type=MESH)
        pl.semaphore_signal(barrier, inc=1, device_id=(me, mod(head + i, 8)), device_id_type=MESH)
        return 0

    lax.fori_loop(1, 8, greet, 0)

    my_k, my_q = k_place(core), q_place(core)

    def lanes(block, width):
        return pl.ds(pl.multiple_of(block * width, width), width)

    fetches = [
        (k_hbm, kv.at[core, my_k, 0]),
        (v_hbm, kv.at[core, my_k, 1]),
        (q_hbm.at[:, lanes(2 * core, ADH)], qs.at[core, my_q, 0]),
        (q_hbm.at[:, lanes(2 * core + 1, ADH)], qs.at[core, my_q, 1]),
        (wt_hbm.at[:, lanes(core, 256)], w.at[core, my_k, my_q]),
        (decay_hbm, decay_ref),
        (b_hbm, b_ref),
        (x_hbm, x_ref),
        (step_hbm, step_ref),
        (c_hbm, c_ref),
        (gate_hbm, gate_ref),
        (skip_hbm, skip_ref),
    ]
    fetches = [pltpu.make_async_copy(src, dst, in_s.at[i]) for i, (src, dst) in enumerate(fetches)]
    for fetch in fetches:
        fetch.start()
    pl.semaphore_wait(barrier, 21)

    def sib_kv(m, place):
        ref = kv.at[m, place]
        return pltpu.make_async_remote_copy(
            src_ref=ref, dst_ref=ref, send_sem=skv_s.at[place], recv_sem=skv_r.at[place],
            device_id=sibling, device_id_type=MESH,
        )

    def sib_q(m, i):
        return pltpu.make_async_remote_copy(
            src_ref=q_hbm.at[:, lanes(2 * (1 - core) + i, ADH)], dst_ref=qs.at[m, q_place(m), i],
            send_sem=sq_s.at[i], recv_sem=sq_r.at[i], device_id=sibling, device_id_type=MESH,
        )

    def sib_w(m):
        return pltpu.make_async_remote_copy(
            src_ref=wt_hbm.at[:, lanes(1 - core, 256)], dst_ref=w.at[m, k_place(m), q_place(m)],
            send_sem=sw_s, recv_sem=sw_r, device_id=sibling, device_id_type=MESH,
        )

    def ring_kv(dr, dist, part, arriving):
        way = 0 if dr > 0 else 1
        place = mod(my_k - dr * (dist if arriving else dist - 1), RING)
        ref = kv.at[core, place, part]
        to = ctx_at(core, my_q, mod(my_k + dr, RING))
        at = (way, dist - 1, part)
        src = (k_hbm, v_hbm)[part] if dist == 1 and not arriving else ref
        return pltpu.make_async_remote_copy(
            src_ref=src, dst_ref=ref, send_sem=kr_s.at[at], recv_sem=kr_r.at[at],
            device_id=(to, head), device_id_type=MESH,
        )

    def ring_q(m, dr, dist, part, arriving):
        way = 0 if dr > 0 else 1
        place = mod(q_place(m) - dr * (dist if arriving else dist - 1), RING)
        ref = qs.at[m, place, part]
        to = ctx_at(m, mod(q_place(m) + dr, RING), k_place(m))
        at = (m, way, dist - 1, part)
        return pltpu.make_async_remote_copy(
            src_ref=ref, dst_ref=ref, send_sem=qr_s.at[at], recv_sem=qr_r.at[at],
            device_id=(to, head), device_id_type=MESH,
        )

    def goes(dr, dist, part):
        return dist < 4 or (dist == 4 and part == (0 if dr > 0 else 1))

    def kv_hop(dist):
        for part in (0, 1):
            for dr in (1, -1):
                if dist > 0 and goes(dr, dist, part):
                    ring_kv(dr, dist, part, True).wait_recv()
                if goes(dr, dist + 1, part):
                    ring_kv(dr, dist + 1, part, False).start()
        if dist > 0:
            for dr in (1, -1) if dist < 4 else (1,):
                sib_kv(core, mod(my_k - dr * dist, RING)).start()

    def q_hop(dist, part):
        for m in (0, 1):
            for dr in (1, -1):
                if dist > 0 and goes(dr, dist, part):
                    ring_q(m, dr, dist, part, True).wait_recv()
                if goes(dr, dist + 1, part):
                    ring_q(m, dr, dist + 1, part, False).start()

    def first(buf, ss, rs, hf, dr, dist, arriving):
        slot = dist - 1 + (0 if dr > 0 else 4)
        block = mod(minor0[hf] - dr * (dist if arriving else dist - 1), RING)
        ref = buf.at[hf, major0[hf], block]
        to = ctx_of(hf, major0[hf], mod(minor0[hf] + dr, RING))
        return pltpu.make_async_remote_copy(
            src_ref=ref, dst_ref=ref, send_sem=ss.at[hf, slot], recv_sem=rs.at[hf, slot],
            device_id=(to, head), device_id_type=MESH,
        )

    def second(buf, ss, rs, hf, dr, dist, pair, arriving):
        way = 0 if dr > 0 else 1
        major = mod(major0[hf] - dr * (dist if arriving else dist - 1), RING)
        two = mod(minor0[hf] // 2 + (0, 1, 3, 2)[pair], RING // 2)
        ref = buf.at[hf, major, pl.ds(2 * two, 2)]
        to = ctx_of(hf, mod(major0[hf] + dr, RING), minor0[hf])
        at = (hf, way, dist - 1, pair)
        return pltpu.make_async_remote_copy(
            src_ref=ref, dst_ref=ref, send_sem=ss.at[at], recv_sem=rs.at[at],
            device_id=(to, head), device_id_type=MESH,
        )

    STREAMS = [(hf, dr) for hf in (0, 1) for dr in (1, -1)]
    reach = {(0, 1): 4, (0, -1): 3, (1, 1): 3, (1, -1): 4}
    w1 = functools.partial(first, w, w1_s, w1_r)
    w2 = functools.partial(second, w, w2_s, w2_r)

    def w_hop(dist):
        for hf, dr in STREAMS:
            if 0 < dist <= reach[hf, dr]:
                w1(hf, dr, dist, True).wait_recv()
            if dist < reach[hf, dr]:
                w1(hf, dr, dist + 1, False).start()

    def w_goes(dr, dist, pair):
        return dist < 4 or (dist == 4 and (pair < 2) == (dr > 0))

    def w_pass(dist, pair):
        for hf, dr in STREAMS:
            if dist > 0 and w_goes(dr, dist, pair):
                w2(hf, dr, dist, pair, True).wait_recv()
            if w_goes(dr, dist + 1, pair):
                w2(hf, dr, dist + 1, pair, False).start()

    kv_hop(0)
    for i in (0, 1):
        sib_q(core, i).start()
    for fetch in fetches[:2]:
        fetch.wait()
    sib_kv(core, my_k).start()
    sib_w(core).start()
    for fetch in fetches[2:5]:
        fetch.wait()

    def weigh(m, i, s, v, fresh):
        n = s.shape[1]
        top = jnp.broadcast_to(jnp.max(s, axis=1, keepdims=True) * SCALE, (TOK, ADH))
        new = top if fresh else jnp.maximum(peak[m, i], top)
        p = jnp.exp2(s * SCALE - jnp.concatenate([new] * (n // ADH), axis=1)).astype(BF)
        pv = dot(p, jnp.concatenate([v, jnp.ones((n, ADH), BF)], axis=1))
        if fresh:
            acc[m, i] = pv
        else:
            shrink = jnp.exp2(peak[m, i] - new)
            acc[m, i] = acc[m, i] * jnp.concatenate([shrink, shrink], axis=1) + pv
        peak[m, i] = new

    rows = lax.broadcasted_iota(jnp.int32, (TOK, TOK), 0)
    cols = lax.broadcasted_iota(jnp.int32, (TOK, TOK), 1)
    causal = rows >= cols

    def own_block(m, _):
        at, q = k_place(m), q_place(m)
        for i in (0, 1):
            s = jnp.where(causal, dot_nt(qs[m, q, i], kv[m, at, 0]), NEG)
            weigh(2 + m, i, s, kv[m, at, 1], True)
        return 0

    def tile(step):
        near_by = 4 - (step + 1) // 2
        away = jnp.where(step % 2 == 1, near_by, mod(RING - near_by, RING))

        def one(m, _):
            q = mod(q_place(m) + away, RING)
            at_z = y + jnp.where(q > z, 1, 0)
            at_y = jnp.where(q > y, RING, jnp.where(q == y, z, 0))
            blocks = jnp.where(m == 0, at_z, at_y)

            t_at = jnp.where(step == 7, 2 + m, m)

            @pl.when(step < 7)
            def _():
                acc[m] = jnp.zeros((2, TOK, 2 * ADH), F32)
                peak[m] = jnp.full((2, TOK, ADH), NEG, F32)

            def keys(t, _):
                ks = kv[m, pl.ds(2 * t, 2), 0].reshape(2 * TOK, ADH)
                vs = kv[m, pl.ds(2 * t, 2), 1].reshape(2 * TOK, ADH)
                both = [dot_nt(qs[m, q, i], ks) for i in (0, 1)]
                for i in (0, 1):
                    weigh(t_at, i, both[i], vs, False)
                return 0

            lax.fori_loop(0, blocks // 2, keys, 0)

            @pl.when(blocks % 2 == 1)
            def _():
                ks, vs = kv[m, blocks - 1, 0], kv[m, blocks - 1, 1]
                both = [dot_nt(qs[m, q, i], ks) for i in (0, 1)]
                for i in (0, 1):
                    weigh(t_at, i, both[i], vs, False)

            for i in (0, 1):
                total = jnp.maximum(acc[t_at, i][:, ADH:], 1e-30)
                part_o[m, away, i] = acc[t_at, i][:, :ADH] / total
                part_l[m, away, i] = peak[t_at, i] + jnp.log2(total)
            return 0

        lax.fori_loop(0, 2, one, 0)

    small = lax.broadcasted_iota(jnp.int32, (ADH, ADH), 0) == lax.broadcasted_iota(jnp.int32, (ADH, ADH), 1)

    def packed(l):
        halves = [l[r * ADH : (r + 1) * ADH] for r in (0, 1)]
        return [jnp.sum(jnp.where(small, half, 0.0), axis=0, keepdims=True) for half in halves]

    def unpacked(block):
        halves = []
        for r in (0, 1):
            row = jnp.broadcast_to(block[r : r + 1], (ADH, ADH))
            column = jnp.sum(jnp.where(small, row, 0.0), axis=1, keepdims=True)
            halves.append(jnp.broadcast_to(column, (ADH, ADH)))
        return jnp.concatenate(halves, axis=0)

    def join(o1, l1, o2, l2):
        top = jnp.maximum(l1, l2)
        w1_, w2_ = jnp.exp2(l1 - top), jnp.exp2(l2 - top)
        total = w1_ + w2_
        return (o1 * w1_ + o2 * w2_) / total, top + jnp.log2(total)

    def back_copies(m, way, k, i):
        at = (m, way, k - 1, i)
        to = ctx_at(m, mod(q_place(m) + (1 if way == 0 else -1), RING), k_place(m))
        return [
            pltpu.make_async_remote_copy(
                src_ref=out.at[at], dst_ref=into.at[at], send_sem=ss.at[at], recv_sem=rs.at[at],
                device_id=(to, head), device_id_type=MESH,
            )
            for out, into, ss, rs in ((tx_o, rx_o, o_s, o_r), (tx_l, rx_l, l_s, l_r))
        ]

    def came(m, way, k, i):
        for copy in back_copies(m, way, k, i):
            copy.wait_recv()
        return rx_o[m, way, k - 1, i].astype(F32), unpacked(rx_l[m, way, k - 1, i])

    def back(k, way, i):
        away = k if way == 0 else RING - k

        def one(m, _):
            o, l = part_o[m, away, i], part_l[m, away, i]
            if k < 3 or (k == 3 and i == way):
                o, l = join(o, l, *came(m, way, k + 1, i))
            tx_o[m, way, k - 1, i] = o.astype(BF)
            tx_l[m, way, k - 1, i] = jnp.concatenate(packed(l) + [jnp.zeros((6, ADH), F32)], axis=0)
            for copy in back_copies(m, way, k, i):
                copy.start()
            return 0

        lax.fori_loop(0, 2, one, 0)

    def collect():
        for i in (0, 1):
            for m in (0, 1):
                o, l = part_o[m, 0, i], part_l[m, 0, i]
                for way in (0, 1):
                    o, l = join(o, l, *came(m, way, 1, i))
                f = 2 * m + i
                heads[:, f * ADH : (f + 1) * ADH] = o.astype(BF)

    lane = lax.broadcasted_iota(jnp.int32, (1, ADH), 1) < 64

    def tri():
        return jnp.where(causal, 1.0, 0.0).astype(F32)

    def spread(pair):
        rows2 = [jnp.broadcast_to(decay_ref[pl.ds(2 * pair + i, 1), :], (64, TOK)) for i in (0, 1)]
        return dot_nt(tri(), jnp.concatenate(rows2, axis=0), lax.Precision.HIGHEST)

    def pair_columns(pair):
        return lanes(pair, ADH)

    def split(vec):
        hi = vec.astype(BF)
        lo = (vec - hi.astype(F32)).astype(BF)
        return jnp.concatenate([jnp.broadcast_to(hi, (8, ADH)), jnp.broadcast_to(lo, (8, ADH))], axis=0)

    def joined(block):
        return block[64:65].astype(F32) + block[72:73].astype(F32)

    def row_copy(out, into, ss, rs, dz, arriving):
        there = mod(z + dz, RING)
        src = mod(z - dz, RING) if arriving else z
        return pltpu.make_async_remote_copy(
            src_ref=out.at[there], dst_ref=into.at[src], send_sem=ss.at[dz], recv_sem=rs.at[dz],
            device_id=(y * RING + there, head), device_id_type=MESH,
        )

    def column_copy(dy, arriving):
        there = mod(y + dy, RING)
        src = mod(y - dy, RING) if arriving else y
        return pltpu.make_async_remote_copy(
            src_ref=tot_out, dst_ref=tot_in.at[src], send_sem=tot_s.at[dy], recv_sem=tot_r.at[dy],
            device_id=(there * RING + z, head), device_id_type=MESH,
        )

    def every(f):
        def one(i, _):
            f(i)
            return 0

        lax.fori_loop(1, RING, one, 0)

    def later(f):
        def one(i, _):
            f(i)
            return 0

        lax.fori_loop(1, RING - y, one, 0)

    def states_out():
        arow[...] = dot_nt(decay_ref[...], tri(), lax.Precision.HIGHEST)
        bt = b_ref[...].astype(F32).T

        def one(pair, _):
            xp = x_ref[:, pair_columns(pair)]
            parts = []
            for i in (0, 1):
                a = arow[pl.ds(2 * pair + i, 1), :]
                tail = jnp.exp(a - a[:, TOK - 1 :]) * step_ref[pl.ds(2 * pair + i, 1), :]
                parts.append(dot((bt * tail).astype(BF), xp))
            state = jnp.where(lane, parts[0], parts[1]).astype(BF)
            last = [arow[pl.ds(2 * pair + i, 1), :][:, TOK - 1 :] for i in (0, 1)]
            through = split(jnp.exp(-jnp.where(lane, last[0], last[1])))
            for i in (0, 1):
                st_out[2 * pair + i, :64] = state[64 * i : 64 * i + 64]
                st_out[2 * pair + i, 64:] = through
            return 0

        lax.fori_loop(0, 4, one, 0)
        st_in[z] = st_out[z]

    def totals_out():
        every(lambda dz: row_copy(st_out, st_in, st_s, st_r, dz, True).wait_recv())

        def one(i, carry):
            state, decay = carry
            pre[i] = state
            predec[i] = jnp.broadcast_to(decay, (8, ADH))
            block = st_in[i]
            t = joined(block)
            return t * state + block[:64].astype(F32), t * decay

        state, decay = lax.fori_loop(0, RING, one, (jnp.zeros((64, ADH), F32), jnp.ones((1, ADH), F32)))
        tot_out[:64] = state.astype(BF)
        tot_out[64:] = split(decay)
        later(lambda dy: column_copy(dy, False).start())

    def incoming_out():
        lax.fori_loop(1, y + 1, lambda dy, _: (column_copy(dy, True).wait_recv(), 0)[1], 0)

        def one(i, state):
            block = tot_in[i]
            return joined(block) * state + block[:64].astype(F32)

        state = lax.fori_loop(0, y, one, jnp.zeros((64, ADH), F32))

        def give(i, _):
            ret_out[i] = (pre[i] + predec[i][:1] * state).astype(BF)
            return 0

        lax.fori_loop(0, RING, give, 0)
        every(lambda dz: row_copy(ret_out, ret_in, ret_s, ret_r, dz, False).start())
        ret_in[z] = ret_out[z]

    def mix_pair(pair):
        if pair == 0:
            every(lambda dz: row_copy(ret_out, ret_in, ret_s, ret_r, dz, True).wait_recv())
            scores[...] = dot_nt(c_ref[...], b_ref[...])
            squares[...] = jnp.zeros_like(squares)

        at = pair_columns(pair)
        xp = x_ref[:, at]
        a_t = spread(pair)
        parts = []
        for i in (0, 1):
            a_u = arow[pl.ds(2 * pair + i, 1), :]
            gap = jnp.where(causal, a_u - a_t[:, 64 * i : 64 * i + 1], NEG)
            mixing = jnp.exp(gap) * (scores[...] * step_ref[pl.ds(2 * pair + i, 1), :])
            parts.append(dot(mixing.astype(BF), xp))
        carried = dot(c_ref[...], ret_in[pl.ds(2 * pair, 2)].reshape(ADH, ADH)) * jnp.exp(-a_t)
        skip = jnp.where(lane, skip_ref[2 * pair], skip_ref[2 * pair + 1])
        total = jnp.where(lane, parts[0], parts[1]) + carried + skip * xp.astype(F32)
        g = gate_ref[:, at].astype(F32)
        total = total * (g / (1.0 + jnp.exp(-g)))
        gated[:, at] = total
        squares[...] += jnp.broadcast_to(jnp.sum(total * total, axis=1, keepdims=True), (TOK, ADH))

    def mix_end():
        norm = lax.rsqrt(squares[...] / 512.0 + 1e-05)
        norm = jnp.concatenate([norm] * 4, axis=1)
        ssm_ref[...] = (gated[...] * norm * gain_ref[...].astype(F32)).astype(BF)

    for i in (0, 1):
        sib_q(1 - core, i).wait_recv()
        if i == 1:
            for fetch in fetches[5:]:
                fetch.wait()
            states_out()
        q_hop(0, i)
    sib_w(1 - core).wait_recv()
    w_hop(0)
    kv_hop(1)
    q_hop(1, 0)
    every(lambda dz: row_copy(st_out, st_in, st_s, st_r, dz, False).start())
    sib_kv(1 - core, k_place(1 - core)).wait_recv()
    lax.fori_loop(0, 2, own_block, 0)
    q_hop(1, 1)
    w_hop(1)
    w_pass(0, 0)
    for dist in (2, 3, 4):
        kv_hop(dist)
        q_hop(dist, 0)
        q_hop(dist, 1)
        w_hop(dist)
        if dist == 3:
            w_pass(0, 1)
            w_pass(0, 2)
            w_pass(1, 0)
            totals_out()
    w_pass(0, 3)
    w_pass(2, 0)

    def rest(i, _):
        sib_kv(1 - core, mod(k_place(1 - core) + i, RING)).wait_recv()
        return 0

    lax.fori_loop(1, RING, rest, 0)

    TURNS = (
        (), ((1, 1),), ((1, 2), (1, 3)), ((3, 0), (2, 1)),
        ((2, 2), (2, 3)), ((4, 0), (3, 1)), ((3, 2), (3, 3)), ((4, 1), (4, 2)),
    )

    def step(i, _):
        for at, turns in enumerate(TURNS):

            @pl.when(i == at)
            def _(turns=turns):
                for turn in turns:
                    w_pass(*turn)

        pl.when(i == 1)(incoming_out)
        tile(i)

        @pl.when(i == 0)
        def _():
            back(4, 0, 0)
            back(4, 1, 1)

        for k in (3, 2, 1):
            for way in (0, 1):

                @pl.when(i == 7 - 2 * k + way)
                def _(k=k, way=way):
                    back(k, way, 1 - way)
                    back(k, way, way)

        return 0

    lax.fori_loop(0, 8, step, 0)
    collect()
    w_pass(4, 3)

    def product(f):
        left = dot_nt(heads[:, :256], w[0, f].reshape(512, 256))
        right = dot_nt(heads[:, 256:], w[1, :, f].reshape(512, 256))
        return (left + right).astype(BF)

    def sib_copy(o):
        return pltpu.make_async_remote_copy(
            src_ref=sib_out.at[o], dst_ref=sib_in.at[o], send_sem=sib_s.at[o], recv_sem=sib_r.at[o],
            device_id=(me, 2 * xc + 1 - core), device_id_type=MESH,
        )

    def side(way):
        return (me, 2 * mod(xc + (1 if way == 0 else -1), XS) + core)

    def x1_copy(way):
        return pltpu.make_async_remote_copy(
            src_ref=x1_out.at[way], dst_ref=x1_in.at[way], send_sem=x1_s.at[way], recv_sem=x1_r.at[way],
            device_id=side(way), device_id_type=MESH,
        )

    def x2_copy(way, part):
        ref = (way, pl.ds(part * HALF, HALF))
        return pltpu.make_async_remote_copy(
            src_ref=x2_out.at[ref], dst_ref=x2_in.at[ref], send_sem=x2_s.at[way, part], recv_sem=x2_r.at[way, part],
            device_id=side(way), device_id_type=MESH,
        )

    def for_sibling(o):
        sib_out[o] = product(2 * mod(xc + o, XS) + 1 - core)
        sib_copy(o).start()

    def for_own(o):
        mine[o] = product(2 * mod(xc + o, XS) + core)

    def both(o, part):
        at = pl.ds(part * HALF, HALF)
        return mine[o, at].astype(F32) + sib_in[o, at].astype(F32)

    for_sibling(2)
    for_own(2)
    for_sibling(1)
    for_sibling(3)
    sib_copy(2).wait_recv()
    for way in (0, 1):
        x1_out[way] = both(2, way).astype(BF)
        x1_copy(way).start()
    for way, o in ((0, 1), (1, 3)):
        for_own(o)
        sib_copy(o).wait_recv()
        x2_out[way, (1 - way) * HALF : (2 - way) * HALF] = both(o, 1 - way).astype(BF)
        x2_copy(way, 1 - way).start()
    mix_pair(0)
    mix_pair(1)
    for way, o in ((0, 1), (1, 3)):
        x1_copy(way).wait_recv()
        x2_out[way, way * HALF : (way + 1) * HALF] = (both(o, way) + x1_in[way].astype(F32)).astype(BF)
        x2_copy(way, way).start()
    for_sibling(0)
    for_own(0)
    mix_pair(2)
    mix_pair(3)
    mix_end()
    sib_copy(0).wait_recv()
    for part in (1, 0):
        x2_copy(0, part).wait_recv()
        x2_copy(1, part).wait_recv()
    for part in (0, 1):
        at = pl.ds(part * HALF, HALF)
        out_ref[at] = (both(0, part) + x2_in[0, at].astype(F32) + x2_in[1, at].astype(F32)).astype(BF)

    def sent(i, _):
        sib_kv(core, i).wait_send()
        return 0

    lax.fori_loop(0, RING, sent, 0)
    for i in (0, 1):
        sib_q(core, i).wait_send()
    sib_w(core).wait_send()
    for k in range(1, 5):
        for way, dr in ((0, 1), (1, -1)):
            for part in (0, 1):
                if goes(dr, k, part):
                    ring_kv(dr, k, part, False).wait_send()

    def sent_both(m, _):
        for k in range(1, 5):
            for way, dr in ((0, 1), (1, -1)):
                for part in (0, 1):
                    if goes(dr, k, part):
                        ring_q(m, dr, k, part, False).wait_send()
                        for copy in back_copies(m, way, k, part):
                            copy.wait_send()
        return 0

    lax.fori_loop(0, 2, sent_both, 0)
    for hf, dr in STREAMS:
        for dist in range(1, reach[hf, dr] + 1):
            w1(hf, dr, dist, False).wait_send()
        for dist in range(1, 5):
            for pair in range(4):
                if w_goes(dr, dist, pair):
                    w2(hf, dr, dist, pair, False).wait_send()
    every(lambda d: row_copy(st_out, st_in, st_s, st_r, d, False).wait_send())
    later(lambda d: column_copy(d, False).wait_send())
    every(lambda d: row_copy(ret_out, ret_in, ret_s, ret_r, d, False).wait_send())
    for o in range(4):
        sib_copy(o).wait_send()
    for way in (0, 1):
        x1_copy(way).wait_send()
        for part in (0, 1):
            x2_copy(way, part).wait_send()


def per_device(
    x_in, gate_z, b_in, c_in, step_size, log_decay, d_skip, norm_gain, query, key, value, o_weight
):
    vmem = pl.BlockSpec(memory_space=pltpu.VMEM)
    hbm = pl.BlockSpec(memory_space=pl.ANY)
    dma = pltpu.SemaphoreType.DMA
    tokens = (TOK, 512)
    return pl.pallas_call(
        kernel,
        out_shape=(jax.ShapeDtypeStruct(tokens, BF), jax.ShapeDtypeStruct(tokens, BF)),
        in_specs=[hbm] * 7 + [vmem] + [hbm] * 4,
        out_specs=(vmem, vmem),
        scratch_shapes=[
            pltpu.VMEM(tokens, BF),
            pltpu.VMEM(tokens, BF),
            pltpu.VMEM((TOK, ADH), BF),
            pltpu.VMEM((TOK, ADH), BF),
            pltpu.VMEM((8, TOK), F32),
            pltpu.VMEM((8, TOK), F32),
            pltpu.SMEM((8,), F32),
            pltpu.VMEM((2, RING, 2, TOK, ADH), BF),
            pltpu.VMEM((2, RING, 2, TOK, ADH), BF),
            pltpu.VMEM((2, RING, RING, 64, 256), BF),
            pltpu.VMEM((4, 2, TOK, 2 * ADH), F32),
            pltpu.VMEM((4, 2, TOK, ADH), F32),
            pltpu.VMEM((2, RING, 2, TOK, ADH), F32),
            pltpu.VMEM((2, RING, 2, TOK, ADH), F32),
            pltpu.VMEM((2, 2, 4, 2, TOK, ADH), BF),
            pltpu.VMEM((2, 2, 4, 2, 8, ADH), F32),
            pltpu.VMEM((2, 2, 4, 2, TOK, ADH), BF),
            pltpu.VMEM((2, 2, 4, 2, 8, ADH), F32),
            pltpu.VMEM(tokens, BF),
            pltpu.VMEM((8, TOK), F32),
            pltpu.VMEM((TOK, TOK), F32),
            pltpu.VMEM(tokens, F32),
            pltpu.VMEM((TOK, ADH), F32),
            pltpu.VMEM((RING, 80, ADH), BF),
            pltpu.VMEM((RING, 80, ADH), BF),
            pltpu.VMEM((RING, 64, ADH), F32),
            pltpu.VMEM((RING, 8, ADH), F32),
            pltpu.VMEM((80, ADH), BF),
            pltpu.VMEM((RING, 80, ADH), BF),
            pltpu.VMEM((RING, 64, ADH), BF),
            pltpu.VMEM((RING, 64, ADH), BF),
            pltpu.VMEM((XS,) + tokens, BF),
            pltpu.VMEM((XS,) + tokens, BF),
            pltpu.VMEM((XS,) + tokens, BF),
            pltpu.VMEM((2, HALF, 512), BF),
            pltpu.VMEM((2, HALF, 512), BF),
            pltpu.VMEM((2,) + tokens, BF),
            pltpu.VMEM((2,) + tokens, BF),
            dma((12,)), dma((8,)), dma((8,)), dma((2,)), dma((2,)), dma, dma, dma((2, 4, 2)), dma((2, 4, 2)),
            *[dma((2, 2, 4, 2))] * 6,
            dma((2, 8)), dma((2, 8)), dma((2, 2, 4, 4)), dma((2, 2, 4, 4)),
            dma((8,)), dma((8,)), dma((8,)), dma((8,)), dma((8,)), dma((8,)),
            dma((4,)), dma((4,)), dma((2,)), dma((2,)), dma((2, 2)), dma((2, 2)),
        ],
        compiler_params=pltpu.CompilerParams(
            collective_id=0, has_side_effects=True, vmem_limit_bytes=60 * 1024 * 1024
        ),
        name="mixer_and_attention",
    )(
        x_in, gate_z, b_in, c_in, step_size, log_decay, d_skip, norm_gain.reshape(1, 512),
        query, key, value, o_weight.T,
    )


def solution(mesh):
    in_specs = (
        P("ctx", "head"),
        P("ctx", "head"),
        P("ctx", "head"),
        P("ctx", "head"),
        P("head", "ctx"),
        P("head", "ctx"),
        P("head"),
        P("head"),
        P("ctx", "head"),
        P("ctx", "head"),
        P("ctx", "head"),
        P("head", "ctx"),
    )
    out_specs = (P("ctx", "head"), P("ctx", "head"))
    return jax.shard_map(
        per_device, mesh=mesh, in_specs=in_specs, out_specs=out_specs, check_vma=False
    )
```
